512 devices in a mesh: dp: 4 (over x), head: 8 (over y, core), seq: 16 (over z).
Axes of the slice: x: 4, y: 4, z: 16, core: 2. Of those that a mesh axis runs over, the one named last changes fastest.
Arguments:
- queries: bfloat16 [32768, 3072], P(('dp', 'seq'), 'head'), parts along dimension 0, may hold values from -58 to 58
- keys: bfloat16 [32768, 3072], P(('dp', 'seq'), 'head'), parts along dimension 0, may hold values from -6 to 6
- values: bfloat16 [32768, 3072], P(('dp', 'seq'), 'head'), parts along dimension 0, may hold values from -16 to 16
- indices: int32 [24, 512, 32], P('head', ('dp', 'seq')), parts along dimension 1, may hold values from 0 to 127, as said below
Outputs:
- attended: bfloat16 [32768, 3072], P(('dp', 'seq'), 'head'), parts along dimension 0
The draws below stay inside these ranges and needn't reach their ends.
There are 4 independent parts, one for each index of `dp`. The reference program is written for one: setup_inputs(seed, part) draws one part's arguments, and reference() takes and returns one part's arrays. A program takes and returns all parts, laid end to end along the dimension named above; each array names one. Nothing has to cross between parts.
Inputs may be any that keep to these rules, and one draw needn't show every extreme that they name: The 32 entries of indices[h, c] are distinct. For one head and the query cubes of one aligned block of 8 cubes, the distinct key cubes they select inside any one aligned block of 8 cubes number at most 3.
All inputs are finite; a program needn't handle non-finite values.
Results may differ from the reference program's by a relative error of at most 0.008.
Values may be sent and summed in bfloat16 or wider, within the bound.
A program may use at most 192 MiB of HBM per device.

```python
import math
import jax
import jax.numpy as jnp
from jax import lax

HEAD_DIM = 128
HEADS = 24
CUBE_TOK = 64
TOPK = 32
CUBE_DEV = 8
CUBES = 128
TOKENS = 8192
LEAST = 2
KEEP = 3
N_SEQ = 16


def selection_table(key):
    base = jax.random.fold_in(key, 101)
    key_count, key_force, key_rank, key_tie = jax.random.split(base, 4)
    counts = jax.random.randint(key_count, (HEADS, N_SEQ, N_SEQ), LEAST, KEEP + 1)
    forced = jax.random.randint(key_force, (HEADS, N_SEQ, 1), 0, N_SEQ)
    is_forced = forced == jnp.arange(N_SEQ, dtype=jnp.int32)[None, None, :]
    counts = jnp.where(is_forced, KEEP, counts)
    raw_rank = jax.random.randint(key_rank, (HEADS, N_SEQ, N_SEQ, CUBE_DEV), 0, 2 ** 16)
    raw_rank = raw_rank * CUBE_DEV + jnp.arange(CUBE_DEV, dtype=jnp.int32)
    ranks = jnp.argsort(jnp.argsort(raw_rank, axis=-1), axis=-1)
    allowed = (ranks < counts[..., None]).astype(jnp.int32).reshape(HEADS, N_SEQ, 1, CUBES)
    favored = jnp.broadcast_to(is_forced[..., None], (HEADS, N_SEQ, N_SEQ, CUBE_DEV))
    favored = favored.astype(jnp.int32).reshape(HEADS, N_SEQ, 1, CUBES)
    leading = (jnp.arange(CUBE_DEV) == 0).astype(jnp.int32)[None, None, :, None]
    breaker = jax.random.randint(key_tie, (HEADS, N_SEQ, CUBE_DEV, CUBES), 0, 2 ** 15)
    breaker = breaker * CUBES + jnp.arange(CUBES, dtype=jnp.int32)
    ranking = allowed * 2 ** 28 + favored * leading * 2 ** 27 + breaker
    _, picks = lax.top_k(ranking, TOPK)
    return picks.reshape(HEADS, CUBES, TOPK).astype(jnp.int32)


def key_table(key):
    base = jax.random.fold_in(key, 202)
    table = jax.random.normal(base, (TOKENS, HEADS * HEAD_DIM), jnp.float32)
    return jnp.clip(table, -6.0, 6.0)


def draw_keys(key, part):
    return key_table(key).astype(jnp.bfloat16)


def draw_indices(key, part):
    return selection_table(key)


def draw_queries(key, part):
    base = jax.random.fold_in(key, 303)
    bound_value = 12.0 + 6000 // HEAD_DIM
    table = 2.0 * jax.random.normal(base, (TOKENS, HEADS * HEAD_DIM), jnp.float32)
    return jnp.clip(table, -bound_value, bound_value).astype(jnp.bfloat16)


def block_levels(own_key, dims, pieces, low, largest):
    gain = 1.0
    for position, blocks in pieces:
        draws = jax.random.uniform(jax.random.fold_in(jax.random.fold_in(own_key, 6), position), (blocks,), jnp.float32, low / len(pieces), largest / len(pieces))
        gain = gain * jnp.repeat(jnp.exp(draws), dims[position] // blocks).reshape((-1,) + (1,) * (len(dims) - 1 - position))
    return gain


def centred(rng, shape, spread, bound, pieces=(), kind=jnp.bfloat16):
    array = spread * jax.random.normal(rng, shape, jnp.float32)
    if pieces:
        array = array * block_levels(rng, shape, pieces, -0.22, 0.18)
    return jnp.clip(array, -bound, bound).astype(kind)


def setup_inputs(seed: int = 0, part: int = 0) -> dict:
    splits = jax.random.split(jax.random.key(seed), 5)
    own_keys = jax.random.split(jax.random.fold_in(splits[4], part), 5)
    queries = draw_queries(jax.random.fold_in(jax.random.fold_in(splits[4], part), 71), part)
    keys = draw_keys(jax.random.fold_in(jax.random.fold_in(splits[4], part), 71), part)
    values = centred(own_keys[2], (TOKENS, HEADS * HEAD_DIM), 3.0, 16.0, ((0, 16), (1, 8)))
    indices = draw_indices(jax.random.fold_in(jax.random.fold_in(splits[4], part), 71), part)
    return {"queries": queries, "keys": keys, "values": values, "indices": indices}


def reference(queries, keys, values, indices):
    heads = indices.shape[0]
    factor = 1.0 / math.sqrt(HEAD_DIM)

    def split_heads(block):
        return block.reshape(CUBES, CUBE_TOK, heads, HEAD_DIM).transpose(2, 0, 1, 3)
    query_heads = split_heads(queries)
    key_heads = split_heads(keys)
    value_heads = split_heads(values)

    def one_head(parts):
        query_one, key_one, value_one, chosen = parts
        key_sets = jnp.take(key_one, chosen.astype(jnp.int32), axis=0)
        value_sets = jnp.take(value_one, chosen.astype(jnp.int32), axis=0)
        scores = jnp.einsum('cqd,cskd->cqsk', query_one.astype(jnp.float32), key_sets.astype(jnp.float32), precision=lax.Precision.HIGHEST) * factor
        highest = lax.optimization_barrier(jnp.max(scores, axis=(2, 3), keepdims=True))
        expo = jnp.exp(scores - highest)
        totals = lax.optimization_barrier(jnp.sum(expo, axis=(2, 3)))
        weights = lax.optimization_barrier(expo.astype(jnp.bfloat16)).astype(jnp.float32)
        mixed = jnp.einsum('cqsk,cskd->cqd', weights, value_sets.astype(jnp.float32), precision=lax.Precision.HIGHEST)
        return (mixed / totals[:, :, None]).astype(jnp.bfloat16)
    result = lax.map(one_head, (query_heads, key_heads, value_heads, indices))
    return result.transpose(1, 2, 0, 3).reshape(CUBES * CUBE_TOK, heads * HEAD_DIM)
```

```python
import functools
import math

import jax
import jax.numpy as jnp
from jax import lax
from jax.experimental import pallas as pl
from jax.experimental.pallas import tpu as pltpu
from jax.sharding import PartitionSpec as P

CUBE_TOK = 64
LANES = 128
MASKED = -1e30
RIGHT, LEFT = 0, 1


def kernel(ring_size, q_hbm, k_hbm, v_hbm, idx_ref, out_ref,
           q_aug, ring, acc, top, tot, q_sem, kv_sem, send_sem, recv_sem):
    heads = idx_ref.shape[0]
    cubes = idx_ref.shape[1]
    picks = idx_ref.shape[2]
    rows = q_hbm.shape[0]
    depth = q_hbm.shape[1] // heads
    half = ring_size // 2
    factor = math.log2(math.e) / math.sqrt(depth)
    me = lax.axis_index("seq")
    right = lax.rem(me + 1, ring_size)
    left = lax.rem(me + ring_size - 1, ring_size)

    barrier = pltpu.get_barrier_semaphore()
    for neighbour in (left, right):
        pl.semaphore_signal(barrier, inc=1, device_id={"seq": neighbour},
                            device_id_type=pl.DeviceIdType.MESH)

    loads = []
    for h in range(heads):
        columns = pl.ds(h * depth, depth)
        for part, ref in ((0, k_hbm), (1, v_hbm)):
            loads.append(pltpu.make_async_copy(
                ref.at[:, columns], ring.at[RIGHT, 0, h, part], kv_sem.at[h, part]))
            loads[-1].start()
    q_loads = []
    for h in range(heads):
        q_loads.append(pltpu.make_async_copy(
            q_hbm.at[:, pl.ds(h * depth, depth)], q_aug.at[h, :, pl.ds(0, depth)], q_sem.at[h]))
        q_loads[-1].start()

    def hop(way, step, h):
        return pltpu.make_async_remote_copy(
            src_ref=ring.at[way, step, h],
            dst_ref=ring.at[way, step + 1, h],
            send_sem=send_sem.at[way, step, h],
            recv_sem=recv_sem.at[way, step, h],
            device_id={"seq": right if way == RIGHT else left},
            device_id_type=pl.DeviceIdType.MESH)

    def first_hop(way, h):
        return pltpu.make_async_remote_copy(
            src_ref=ring.at[RIGHT, 0, h],
            dst_ref=ring.at[way, 1, h],
            send_sem=send_sem.at[way, 0, h],
            recv_sem=recv_sem.at[way, 0, h],
            device_id={"seq": right if way == RIGHT else left},
            device_id_type=pl.DeviceIdType.MESH)

    def last_hop(way, h):
        part = 0 if way == RIGHT else 1
        return pltpu.make_async_remote_copy(
            src_ref=ring.at[way, half - 1, h, part],
            dst_ref=ring.at[way, half, h, part],
            send_sem=send_sem.at[way, half - 1, h],
            recv_sem=recv_sem.at[way, half - 1, h],
            device_id={"seq": right if way == RIGHT else left},
            device_id_type=pl.DeviceIdType.MESH)

    pl.semaphore_wait(barrier, 2)
    for h in range(heads):
        loads[2 * h].wait()
        loads[2 * h + 1].wait()
        first_hop(RIGHT, h).start()
        first_hop(LEFT, h).start()

    lanes = lax.broadcasted_iota(jnp.int32, (cubes, LANES), 1)
    for h in range(heads):
        chosen = idx_ref[h]
        hit = jnp.zeros((cubes, LANES), jnp.float32)
        for j in range(picks):
            hit = jnp.where(chosen[:, j:j + 1] == lanes, 1.0, hit)
        bias = jnp.where(hit > 0.5, 0.0, MASKED)
        for c in range(cubes):
            q_aug[h, c * CUBE_TOK:(c + 1) * CUBE_TOK, depth:] = jnp.broadcast_to(
                bias[c:c + 1, :], (CUBE_TOK, LANES)).astype(q_aug.dtype)
    top[...] = jnp.full(top.shape, MASKED, jnp.float32)
    tot[...] = jnp.zeros(tot.shape, jnp.float32)
    acc[...] = jnp.zeros(acc.shape, jnp.float32)
    for h in range(heads):
        q_loads[h].wait()

    key_cube = lax.shift_right_logical(
        lax.broadcasted_iota(jnp.int32, (rows, LANES), 0), jnp.int32(6))
    key_lane = lax.broadcasted_iota(jnp.int32, (rows, LANES), 1)

    def one_hot(owner):
        return jnp.where(key_lane == key_cube + owner * cubes, 1.0, 0.0).astype(jnp.bfloat16)

    tile = min(rows, 256)

    def attend(h, blocks):
        wide = [jnp.concatenate([key[...], hot], axis=1) for key, _, hot in blocks]
        for r in range(0, rows, tile):
            part = pl.ds(r, tile)
            scores = [
                lax.dot_general(q_aug[h, part, :], k, (((1,), (1,)), ((), ())),
                                preferred_element_type=jnp.float32)
                for k in wide
            ]
            peak = jnp.max(functools.reduce(jnp.maximum, scores), axis=1, keepdims=True)
            before = top[h, part, :]
            after = jnp.maximum(before, peak)
            scale = jnp.exp2((before - after) * factor)
            total = tot[h, part, :] * scale
            mixed = acc[h, part, :] * scale
            for s, (_, value, _) in zip(scores, blocks):
                pieces = []
                for c in range(0, s.shape[1], LANES):
                    w = jnp.exp2((s[:, c:c + LANES] - after) * factor)
                    total = total + w
                    pieces.append(w.astype(jnp.bfloat16))
                mixed = mixed + jnp.dot(jnp.concatenate(pieces, axis=1), value[...],
                                        preferred_element_type=jnp.float32)
            top[h, part, :] = after
            tot[h, part, :] = total
            acc[h, part, :] = mixed

    hot_own = one_hot(me)
    for h in range(heads):
        attend(h, [(ring.at[RIGHT, 0, h, 0], ring.at[RIGHT, 0, h, 1], hot_own)])

    def body(step, carry):
        hot_r = one_hot(lax.rem(me - step + ring_size, ring_size))
        hot_l = one_hot(lax.rem(me + step, ring_size))
        for h in range(heads):
            for way in (RIGHT, LEFT):
                hop(way, step - 1, h).wait_recv()

                @pl.when(step < half - 1)
                def _():
                    hop(way, step, h).start()

                @pl.when(step == half - 1)
                def _():
                    last_hop(way, h).start()

            attend(h, [
                (ring.at[RIGHT, step, h, 0], ring.at[RIGHT, step, h, 1], hot_r),
                (ring.at[LEFT, step, h, 0], ring.at[LEFT, step, h, 1], hot_l),
            ])
        return carry

    lax.fori_loop(1, half, body, 0)

    hot_far = one_hot(lax.rem(me + half, ring_size))
    for h in range(heads):
        last_hop(RIGHT, h).wait_recv()
        last_hop(LEFT, h).wait_recv()
        attend(h, [(ring.at[RIGHT, half, h, 0], ring.at[LEFT, half, h, 1], hot_far)])
        total = jnp.sum(tot[h], axis=1, keepdims=True)
        out_ref[:, h * depth:(h + 1) * depth] = (acc[h] / total).astype(out_ref.dtype)

    for way in (RIGHT, LEFT):
        for h in range(heads):
            first_hop(way, h).wait_send()
            last_hop(way, h).wait_send()

    def drain(step, carry):
        for way in (RIGHT, LEFT):
            for h in range(heads):
                hop(way, step, h).wait_send()
        return carry

    lax.fori_loop(1, half - 1, drain, 0)


def body(ring_size, queries, keys, values, indices):
    heads = indices.shape[0]
    rows, width = queries.shape
    depth = width // heads
    half = ring_size // 2
    vmem = pl.BlockSpec(memory_space=pltpu.VMEM)
    hbm = pl.BlockSpec(memory_space=pl.ANY)
    return pl.pallas_call(
        functools.partial(kernel, ring_size),
        out_shape=jax.ShapeDtypeStruct((rows, width), queries.dtype),
        in_specs=[hbm, hbm, hbm, vmem],
        out_specs=vmem,
        scratch_shapes=[
            pltpu.VMEM((heads, rows, depth + LANES), jnp.bfloat16),
            pltpu.VMEM((2, half + 1, heads, 2, rows, depth), jnp.bfloat16),
            pltpu.VMEM((heads, rows, depth), jnp.float32),
            pltpu.VMEM((heads, rows, LANES), jnp.float32),
            pltpu.VMEM((heads, rows, LANES), jnp.float32),
            pltpu.SemaphoreType.DMA((heads,)),
            pltpu.SemaphoreType.DMA((heads, 2)),
            pltpu.SemaphoreType.DMA((2, half, heads)),
            pltpu.SemaphoreType.DMA((2, half, heads)),
        ],
        compiler_params=pltpu.CompilerParams(
            collective_id=0, has_side_effects=True, vmem_limit_bytes=48 * 2 ** 20),
        cost_estimate=pl.CostEstimate(
            flops=4 * rows * rows * ring_size * width,
            bytes_accessed=8 * rows * width,
            transcendentals=rows * rows * ring_size * heads),
        name="ring_attention",
    )(queries, keys, values, indices)


def solution(mesh):
    placed = (
        P(("dp", "seq"), "head"),
        P(("dp", "seq"), "head"),
        P(("dp", "seq"), "head"),
        P("head", ("dp", "seq"), None),
    )
    return jax.shard_map(
        functools.partial(body, mesh.shape["seq"]), mesh=mesh, in_specs=placed,
        out_specs=P(("dp", "seq"), "head"), check_vma=False,
    )
```

```python
import functools
import math

import jax
import jax.numpy as jnp
from jax import lax
from jax.experimental import pallas as pl
from jax.experimental.pallas import tpu as pltpu
from jax.sharding import PartitionSpec as P

CUBE_TOK = 64
LANES = 128
MASKED = -1e30
KEEP = 3
PICKED = 16
NEAR = (1, -1, 2, -2)
RIGHT, LEFT = 0, 1
SHORT, LONG = 0, 1


def kernel(ring_size, q_hbm, k_hbm, v_hbm, idx_hbm, out_ref,
           q_aug, ring, stage, pairs, single, marks, tables, idx_ref, acc, top, tot,
           q_sem, kv_sem, idx_sem, mark_send, mark_recv, full_send, full_recv, pack_send, pack_recv):
    heads, cubes, picks = idx_ref.shape
    rows = q_hbm.shape[0]
    depth = q_hbm.shape[1] // heads
    half = ring_size // 2
    whole = half - 3
    factor = math.log2(math.e) / math.sqrt(depth)
    me = lax.axis_index("seq")

    def away(distance):
        return lax.rem(me + distance + ring_size, ring_size)

    def source(way, distance):
        return away(-distance if way == RIGHT else distance)

    def target(way):
        return {"seq": away(1 if way == RIGHT else -1)}

    barrier = pltpu.get_barrier_semaphore()
    for distance in (1, -1, 2, -2):
        pl.semaphore_signal(barrier, inc=1, device_id={"seq": away(distance)},
                            device_id_type=pl.DeviceIdType.MESH)

    idx_load = pltpu.make_async_copy(idx_hbm, idx_ref, idx_sem)
    idx_load.start()
    loads = []
    for h in range(heads):
        columns = pl.ds(h * depth, depth)
        for part, ref in ((0, k_hbm), (1, v_hbm)):
            loads.append(pltpu.make_async_copy(
                ref.at[:, columns], ring.at[RIGHT, 0, h, part], kv_sem.at[h, part]))
            loads[-1].start()
    q_loads = []
    for h in range(heads):
        q_loads.append(pltpu.make_async_copy(
            q_hbm.at[:, pl.ds(h * depth, depth)], q_aug.at[h, :, pl.ds(0, depth)], q_sem.at[h]))
        q_loads[-1].start()

    def remote(src, dst, sends, recvs, device):
        return pltpu.make_async_remote_copy(
            src_ref=src, dst_ref=dst, send_sem=sends, recv_sem=recvs,
            device_id=device, device_id_type=pl.DeviceIdType.MESH)

    def hop(way, step, h):
        first = isinstance(step, int) and step == 0
        return remote(ring.at[RIGHT if first else way, step, h], ring.at[way, step + 1, h],
                      full_send.at[way, step, h], full_recv.at[way, step, h], target(way))

    def long_part(way):
        return 0 if way == RIGHT else 1

    def whole_long(way, h):
        part = long_part(way)
        return remote(ring.at[way, whole, h, part], ring.at[way, whole + 1, h, part],
                      full_send.at[way, whole, h], full_recv.at[way, whole, h], target(way))

    def pair_hop(way, kind, h):
        return remote(stage.at[way, kind, h], pairs.at[way, kind, h],
                      pack_send.at[way, kind, h, 0], pack_recv.at[way, kind, h, 0], target(way))

    def single_hop(way, kind, h):
        return remote(pairs.at[way, kind, h, 1], single.at[way, kind, h],
                      pack_send.at[way, kind, h, 1], pack_recv.at[way, kind, h, 1], target(way))

    def mark_hop(n):
        return remote(marks.at[0], marks.at[1 + (n ^ 1)], mark_send.at[n], mark_recv.at[n],
                      {"seq": away(NEAR[n])})

    pl.semaphore_wait(barrier, 4)
    for h in range(heads):
        loads[2 * h].wait()
        loads[2 * h + 1].wait()
        hop(RIGHT, 0, h).start()
        hop(LEFT, 0, h).start()

    lanes = lax.broadcasted_iota(jnp.int32, (cubes, LANES), 1)
    idx_load.wait()
    marks[0] = jnp.zeros(marks.shape[1:], jnp.float32)
    for h in range(heads):
        chosen = idx_ref[h]
        hit = jnp.zeros((cubes, LANES), jnp.float32)
        for j in range(picks):
            hit = jnp.where(chosen[:, j:j + 1] == lanes, 1.0, hit)
        marks[0, h:h + 1, :] = jnp.max(hit, axis=0, keepdims=True)
        bias = jnp.where(hit > 0.5, 0.0, MASKED)
        for c in range(cubes):
            q_aug[h, c * CUBE_TOK:(c + 1) * CUBE_TOK, depth:] = jnp.broadcast_to(
                bias[c:c + 1, :], (CUBE_TOK, LANES)).astype(q_aug.dtype)
    for n in range(len(NEAR)):
        mark_hop(n).start()
    top[...] = jnp.full(top.shape, MASKED, jnp.float32)
    tot[...] = jnp.zeros(tot.shape, jnp.float32)
    acc[...] = jnp.zeros(acc.shape, jnp.float32)

    shift = lax.shift_right_logical
    key_cube = shift(lax.broadcasted_iota(jnp.int32, (rows, LANES), 0), jnp.int32(6))
    key_lane = lax.broadcasted_iota(jnp.int32, (rows, LANES), 1)

    def one_hot(owner):
        return jnp.where(key_lane == key_cube + owner * cubes, 1.0, 0.0).astype(jnp.bfloat16)

    tile = min(rows, 256)

    def attend(h, blocks):
        for r in range(0, rows, tile):
            part = pl.ds(r, tile)
            scores = [
                lax.dot_general(q_aug[h, part, :], key, (((1,), (1,)), ((), ())),
                                preferred_element_type=jnp.float32)
                for key, _ in blocks
            ]
            peak = functools.reduce(
                jnp.maximum, [jnp.max(s, axis=1, keepdims=True) for s in scores])
            before = top[h, part, :]
            after = jnp.maximum(before, peak)
            scale = jnp.exp2((before - after) * factor)
            total = tot[h, part, :] * scale
            mixed = acc[h, part, :] * scale
            for s, (_, value) in zip(scores, blocks):
                pieces = []
                for c in range(0, s.shape[1], LANES):
                    w = jnp.exp2((s[:, c:c + LANES] - after) * factor)
                    total = total + w
                    pieces.append(w.astype(jnp.bfloat16))
                mixed = mixed + jnp.dot(jnp.concatenate(pieces, axis=1), value,
                                        preferred_element_type=jnp.float32)
            top[h, part, :] = after
            tot[h, part, :] = total
            acc[h, part, :] = mixed

    def whole_block(way, step, h, hot):
        return (jnp.concatenate([ring[way, step, h, 0], hot], axis=1), ring[way, step, h, 1])

    for h in range(heads):
        q_loads[h].wait()
    hot_own = one_hot(me)
    for h in range(heads):
        attend(h, [whole_block(RIGHT, 0, h, hot_own)])

    across = lax.broadcasted_iota(jnp.int32, (LANES, LANES), 1)
    down = lax.broadcasted_iota(jnp.int32, (LANES, LANES), 0)
    same = shift(across, jnp.int32(3)) == shift(down, jnp.int32(3))
    before_it = jnp.where(same & (down < across), 1.0, 0.0).astype(jnp.bfloat16)
    rank_row = jnp.dot(marks[0].astype(jnp.bfloat16), before_it, preferred_element_type=jnp.float32)
    mark_row = marks[0]
    weight = jnp.where(same & (across < down), 1.0, jnp.where(across == down, float(PICKED), 0.0))
    ones = jnp.ones((LANES, LANES), jnp.bfloat16)
    for n in range(len(NEAR)):
        mark_hop(n).wait_recv()
    for n in range(1 + len(NEAR)):
        for h in range(heads):
            tables[n, h] = jnp.dot((weight * marks[n, h:h + 1, :]).astype(jnp.bfloat16), ones,
                                   preferred_element_type=jnp.float32)

    def pick(n, h, owner, block):
        table = tables[n, h, pl.ds(pl.multiple_of(owner * cubes, cubes), cubes), :]
        out = [jnp.zeros((CUBE_TOK, depth), jnp.float32) for _ in range(KEEP)]
        for c in range(cubes):
            cube = block[c * CUBE_TOK:(c + 1) * CUBE_TOK, :].astype(jnp.float32)
            for r in range(KEEP):
                out[r] = jnp.where(table[c:c + 1, :] == float(PICKED + r), cube, out[r])
        return jnp.concatenate(out, axis=0).astype(jnp.bfloat16)

    lane = lax.broadcasted_iota(jnp.int32, (1, LANES), 1)

    def pack_hot(h, owner):
        inside = (shift(lane, jnp.int32(3)) == owner) & (mark_row[h:h + 1, :] > 0.5)
        out = []
        for r in range(KEEP):
            hot = jnp.where(inside & (rank_row[h:h + 1, :] == float(r)), 1.0, 0.0)
            found = jnp.max(hot, axis=1, keepdims=True)
            out.append(jnp.broadcast_to(jnp.where(found > 0.5, hot, 1.0), (CUBE_TOK, LANES)))
        return jnp.concatenate(out, axis=0).astype(jnp.bfloat16)

    def make_packs(way, kind, h, distance, part):
        owner = source(way, distance)
        block = ring[way, distance, h, part]
        first = 1 if way == RIGHT else 2
        stage[way, kind, h, 0] = pick(first, h, owner, block)
        stage[way, kind, h, 1] = pick(first + 2, h, owner, block)

    def body(step, carry):
        hots = [one_hot(source(way, step)) for way in (RIGHT, LEFT)]
        for h in range(heads):
            for way in (RIGHT, LEFT):
                hop(way, step - 1, h).wait_recv()
                hop(way, step, h).start()
            attend(h, [whole_block(way, step, h, hots[way]) for way in (RIGHT, LEFT)])
        return carry

    lax.fori_loop(1, whole, body, 0)

    hots = [one_hot(source(way, whole)) for way in (RIGHT, LEFT)]
    for h in range(heads):
        for way in (RIGHT, LEFT):
            hop(way, whole - 1, h).wait_recv()
            whole_long(way, h).start()
        for way in (RIGHT, LEFT):
            make_packs(way, SHORT, h, whole, 1 - long_part(way))
            pair_hop(way, SHORT, h).start()
        attend(h, [whole_block(way, whole, h, hots[way]) for way in (RIGHT, LEFT)])

    for h in range(heads):
        for way in (RIGHT, LEFT):
            whole_long(way, h).wait_recv()
            make_packs(way, LONG, h, whole + 1, long_part(way))
            pair_hop(way, LONG, h).start()
            pair_hop(way, SHORT, h).wait_recv()
            single_hop(way, SHORT, h).start()
        far_right, far_left = source(RIGHT, whole + 1), source(LEFT, whole + 1)
        keys = jnp.concatenate([pick(0, h, far_right, ring[RIGHT, whole + 1, h, 0]),
                                pairs[LEFT, SHORT, h, 0]], axis=0)
        hot = jnp.concatenate([pack_hot(h, far_right), pack_hot(h, far_left)], axis=0)
        values = jnp.concatenate([pairs[RIGHT, SHORT, h, 0],
                                  pick(0, h, far_left, ring[LEFT, whole + 1, h, 1])], axis=0)
        attend(h, [(jnp.concatenate([keys, hot], axis=1), values)])

    for h in range(heads):
        for way in (RIGHT, LEFT):
            pair_hop(way, LONG, h).wait_recv()
            single_hop(way, LONG, h).start()
            single_hop(way, SHORT, h).wait_recv()
        keys = jnp.concatenate([pairs[RIGHT, LONG, h, 0], single[LEFT, SHORT, h]], axis=0)
        hot = jnp.concatenate([pack_hot(h, source(RIGHT, whole + 2)),
                               pack_hot(h, source(LEFT, whole + 2))], axis=0)
        values = jnp.concatenate([single[RIGHT, SHORT, h], pairs[LEFT, LONG, h, 0]], axis=0)
        attend(h, [(jnp.concatenate([keys, hot], axis=1), values)])

    empty = jnp.zeros((CUBE_TOK, depth), jnp.bfloat16)
    for h in range(heads):
        hot = jnp.concatenate([pack_hot(h, away(half)), jnp.ones((CUBE_TOK, LANES), jnp.bfloat16)], axis=0)
        single_hop(RIGHT, LONG, h).wait_recv()
        single_hop(LEFT, LONG, h).wait_recv()
        keys = jnp.concatenate([single[RIGHT, LONG, h], empty], axis=0)
        values = jnp.concatenate([single[LEFT, LONG, h], empty], axis=0)
        attend(h, [(jnp.concatenate([keys, hot], axis=1), values)])
        total = jnp.sum(tot[h], axis=1, keepdims=True)
        out_ref[:, h * depth:(h + 1) * depth] = (acc[h] / total).astype(out_ref.dtype)

    for n in range(len(NEAR)):
        mark_hop(n).wait_send()
    for h in range(heads):
        for way in (RIGHT, LEFT):
            hop(way, 0, h).wait_send()
            whole_long(way, h).wait_send()
            for kind in (SHORT, LONG):
                pair_hop(way, kind, h).wait_send()
                single_hop(way, kind, h).wait_send()

    def drain(step, carry):
        for way in (RIGHT, LEFT):
            for h in range(heads):
                hop(way, step, h).wait_send()
        return carry

    lax.fori_loop(1, whole, drain, 0)


def body(ring_size, queries, keys, values, indices):
    heads, cubes, picks = indices.shape
    rows, width = queries.shape
    depth = width // heads
    half = ring_size // 2
    pack = KEEP * CUBE_TOK
    hbm = pl.BlockSpec(memory_space=pl.ANY)
    return pl.pallas_call(
        functools.partial(kernel, ring_size),
        out_shape=jax.ShapeDtypeStruct((rows, width), queries.dtype),
        in_specs=[hbm] * 4,
        out_specs=pl.BlockSpec(memory_space=pltpu.VMEM),
        scratch_shapes=[
            pltpu.VMEM((heads, rows, depth + LANES), jnp.bfloat16),
            pltpu.VMEM((2, half - 1, heads, 2, rows, depth), jnp.bfloat16),
            pltpu.VMEM((2, 2, heads, 2, pack, depth), jnp.bfloat16),
            pltpu.VMEM((2, 2, heads, 2, pack, depth), jnp.bfloat16),
            pltpu.VMEM((2, 2, heads, pack, depth), jnp.bfloat16),
            pltpu.VMEM((1 + len(NEAR), 8, LANES), jnp.float32),
            pltpu.VMEM((1 + len(NEAR), heads, LANES, LANES), jnp.float32),
            pltpu.VMEM((heads, cubes, picks), jnp.int32),
            pltpu.VMEM((heads, rows, depth), jnp.float32),
            pltpu.VMEM((heads, rows, LANES), jnp.float32),
            pltpu.VMEM((heads, rows, LANES), jnp.float32),
            pltpu.SemaphoreType.DMA((heads,)),
            pltpu.SemaphoreType.DMA((heads, 2)),
            pltpu.SemaphoreType.DMA,
            pltpu.SemaphoreType.DMA((len(NEAR),)),
            pltpu.SemaphoreType.DMA((len(NEAR),)),
            pltpu.SemaphoreType.DMA((2, half - 2, heads)),
            pltpu.SemaphoreType.DMA((2, half - 2, heads)),
            pltpu.SemaphoreType.DMA((2, 2, heads, 2)),
            pltpu.SemaphoreType.DMA((2, 2, heads, 2)),
        ],
        compiler_params=pltpu.CompilerParams(
            collective_id=0, has_side_effects=True, vmem_limit_bytes=63 * 2 ** 20),
        cost_estimate=pl.CostEstimate(
            flops=4 * rows * rows * ring_size * width,
            bytes_accessed=8 * rows * width,
            transcendentals=rows * rows * ring_size * heads),
        name="ring_attention",
    )(queries, keys, values, indices)


def solution(mesh):
    placed = (
        P(("dp", "seq"), "head"),
        P(("dp", "seq"), "head"),
        P(("dp", "seq"), "head"),
        P("head", ("dp", "seq"), None),
    )
    return jax.shard_map(
        functools.partial(body, mesh.shape["seq"]), mesh=mesh, in_specs=placed,
        out_specs=P(("dp", "seq"), "head"), check_vma=False,
    )
```

```python
import functools
import math

import jax
import jax.numpy as jnp
from jax import lax
from jax.experimental import pallas as pl
from jax.experimental.pallas import tpu as pltpu
from jax.sharding import PartitionSpec as P

CUBE_TOK = 64
LIMIT = 53 * 2 ** 20 + 2 ** 19
LANES = 128
MASKED = -1e30
KEEP = 3
PICKED = 16
NEAR = (1, -1, 2, -2)
RIGHT, LEFT = 0, 1
K, V = 0, 1
SHORT, LONG = 0, 1
FAR_RIGHT = ((0xFDFF, 0xFDFF, 0xFDFF), (0x0080, 0x0080, 0x0080))


def kernel(ring_size, q_hbm, k_hbm, v_hbm, idx_hbm, out_ref,
           q_aug, ring, stage, pairs, single, mine, marks, tables, idx_ref, acc, top, tot,
           q_sem, kv_sem, idx_sem, mark_send, mark_recv, full_send, full_recv, pack_send, pack_recv):
    heads, cubes, picks = idx_ref.shape
    rows = q_hbm.shape[0]
    depth = q_hbm.shape[1] // heads
    half = ring_size // 2
    whole = half - 3
    factor = math.log2(math.e) / math.sqrt(depth)
    me = lax.axis_index("seq")

    def away(distance):
        return lax.rem(me + distance + ring_size, ring_size)

    def source(way, distance):
        return away(-distance if way == RIGHT else distance)

    def target(way):
        return {"seq": away(1 if way == RIGHT else -1)}

    barrier = pltpu.get_barrier_semaphore()
    for distance in (1, -1):
        pl.semaphore_signal(barrier, inc=1, device_id={"seq": away(distance)},
                            device_id_type=pl.DeviceIdType.MESH)

    idx_load = pltpu.make_async_copy(idx_hbm, idx_ref, idx_sem)
    idx_load.start()
    loads = []
    for h in range(heads):
        columns = pl.ds(h * depth, depth)
        for part, ref in ((0, k_hbm), (1, v_hbm)):
            loads.append(pltpu.make_async_copy(
                ref.at[:, columns], ring.at[RIGHT, 0, h, part], kv_sem.at[h, part]))
            loads[-1].start()
    q_loads = []
    for h in range(heads):
        q_loads.append(pltpu.make_async_copy(
            q_hbm.at[:, pl.ds(h * depth, depth)], q_aug.at[h, :, pl.ds(0, depth)], q_sem.at[h]))
        q_loads[-1].start()

    def remote(src, dst, sends, recvs, device):
        return pltpu.make_async_remote_copy(
            src_ref=src, dst_ref=dst, send_sem=sends, recv_sem=recvs,
            device_id=device, device_id_type=pl.DeviceIdType.MESH)

    def hop(way, step, h):
        first = isinstance(step, int) and step == 0
        return remote(ring.at[RIGHT if first else way, step, h], ring.at[way, step + 1, h],
                      full_send.at[way, step, h], full_recv.at[way, step, h], target(way))

    def goes_far(way, part, h, owner):
        bit = lax.rem(lax.shift_right_logical(jnp.int32(FAR_RIGHT[part][h]), owner), 2)
        return bit == (1 if way == RIGHT else 0)

    def whole_part(way, part, h):
        return remote(ring.at[way, whole, h, part], ring.at[way, whole + 1, h, part],
                      pack_send.at[way, part, h, 2], pack_recv.at[way, part, h, 2], target(way))

    def pair_hop(way, part, kind, h):
        return remote(stage.at[way, part, kind, h], pairs.at[way, part, kind, h],
                      pack_send.at[way, part, h, kind], pack_recv.at[way, part, h, kind], target(way))

    def single_hop(way, part, kind, h):
        return remote(pairs.at[way, part, kind, h, 1], single.at[way, part, kind, h],
                      pack_send.at[way, part, h, 3 + kind], pack_recv.at[way, part, h, 3 + kind], target(way))

    def mark_hop(n):
        return remote(marks.at[0 if n < 2 else 1 + ((n - 2) ^ 1)], marks.at[1 + (n ^ 1)],
                      mark_send.at[n], mark_recv.at[n], {"seq": away(NEAR[n % 2])})

    pl.semaphore_wait(barrier, 2)
    for h in range(heads):
        loads[2 * h].wait()
        loads[2 * h + 1].wait()
        hop(RIGHT, 0, h).start()
        hop(LEFT, 0, h).start()

    lanes = lax.broadcasted_iota(jnp.int32, (cubes, LANES), 1)
    idx_load.wait()
    marks[0] = jnp.zeros(marks.shape[1:], jnp.float32)
    for h in range(heads):
        chosen = idx_ref[h]
        hit = jnp.zeros((cubes, LANES), jnp.float32)
        for j in range(picks):
            hit = jnp.where(chosen[:, j:j + 1] == lanes, 1.0, hit)
        marks[0, h:h + 1, :] = jnp.max(hit, axis=0, keepdims=True)
        bias = jnp.where(hit > 0.5, 0.0, MASKED)
        for c in range(cubes):
            q_aug[h, c * CUBE_TOK:(c + 1) * CUBE_TOK, depth:] = jnp.broadcast_to(
                bias[c:c + 1, :], (CUBE_TOK, LANES)).astype(q_aug.dtype)
    for n in (0, 1):
        mark_hop(n).start()
    top[...] = jnp.full(top.shape, MASKED, jnp.float32)
    tot[...] = jnp.zeros(tot.shape, jnp.float32)
    acc[...] = jnp.zeros(acc.shape, jnp.float32)

    shift = lax.shift_right_logical
    key_cube = shift(lax.broadcasted_iota(jnp.int32, (rows, LANES), 0), jnp.int32(6))
    key_lane = lax.broadcasted_iota(jnp.int32, (rows, LANES), 1)

    def one_hot(owner):
        return jnp.where(key_lane == key_cube + owner * cubes, 1.0, 0.0).astype(jnp.bfloat16)

    tile = min(rows, 256)

    def attend(h, blocks):
        for r in range(0, rows, tile):
            part = pl.ds(r, tile)
            scores = [
                lax.dot_general(q_aug[h, part, :], key, (((1,), (1,)), ((), ())),
                                preferred_element_type=jnp.float32)
                for key, _ in blocks
            ]
            peak = functools.reduce(
                jnp.maximum, [jnp.max(s, axis=1, keepdims=True) for s in scores])
            before = top[h, part, :]
            after = jnp.maximum(before, peak)
            scale = jnp.exp2((before - after) * factor)
            total = tot[h, part, :] * scale
            mixed = acc[h, part, :] * scale
            for s, (_, value) in zip(scores, blocks):
                pieces = []
                for c in range(0, s.shape[1], LANES):
                    w = jnp.exp2((s[:, c:c + LANES] - after) * factor)
                    total = total + w
                    pieces.append(w.astype(jnp.bfloat16))
                mixed = mixed + jnp.dot(jnp.concatenate(pieces, axis=1), value,
                                        preferred_element_type=jnp.float32)
            top[h, part, :] = after
            tot[h, part, :] = total
            acc[h, part, :] = mixed

    def whole_block(way, step, h, hot):
        return (jnp.concatenate([ring[way, step, h, 0], hot], axis=1), ring[way, step, h, 1])

    for h in range(heads):
        q_loads[h].wait()
    hot_own = one_hot(me)
    for h in range(heads):
        attend(h, [whole_block(RIGHT, 0, h, hot_own)])

    def pick(n, h, owner, block):
        table = tables[n, h, pl.ds(pl.multiple_of(owner * cubes, cubes), cubes), :]
        out = [jnp.zeros((CUBE_TOK, depth), jnp.float32) for _ in range(KEEP)]
        for c in range(cubes):
            cube = block[c * CUBE_TOK:(c + 1) * CUBE_TOK, :].astype(jnp.float32)
            for r in range(KEEP):
                out[r] = jnp.where(table[c:c + 1, :] == float(PICKED + r), cube, out[r])
        return jnp.concatenate(out, axis=0).astype(jnp.bfloat16)

    lane = lax.broadcasted_iota(jnp.int32, (1, LANES), 1)

    def pack_hot(h, owner):
        inside = (shift(lane, jnp.int32(3)) == owner) & (mark_row[h:h + 1, :] > 0.5)
        out = []
        for r in range(KEEP):
            hot = jnp.where(inside & (rank_row[h:h + 1, :] == float(r)), 1.0, 0.0)
            found = jnp.max(hot, axis=1, keepdims=True)
            out.append(jnp.broadcast_to(jnp.where(found > 0.5, hot, 1.0), (CUBE_TOK, LANES)))
        return jnp.concatenate(out, axis=0).astype(jnp.bfloat16)

    def make_packs(way, part, kind, h, distance):
        owner = source(way, distance)
        block = ring[way, distance, h, part]
        first = 1 if way == RIGHT else 2
        stage[way, part, kind, h, 0] = pick(first, h, owner, block)
        stage[way, part, kind, h, 1] = pick(first + 2, h, owner, block)

    def either(condition, first, second):
        pl.when(condition)(first)
        pl.when(jnp.logical_not(condition))(second)

    def attend_packs(h, near, far):
        keys = jnp.concatenate([mine[RIGHT, K], mine[LEFT, K]], axis=0)
        values = jnp.concatenate([mine[RIGHT, V], mine[LEFT, V]], axis=0)
        hot = jnp.concatenate([pack_hot(h, near), pack_hot(h, far)], axis=0)
        attend(h, [(jnp.concatenate([keys, hot], axis=1), values)])

    def body(step, carry):
        @pl.when(step == 2)
        def _():
            for n in (0, 1):
                mark_hop(n).wait_recv()
            for n in (2, 3):
                mark_hop(n).start()

        hots = [one_hot(source(way, step)) for way in (RIGHT, LEFT)]
        for h in range(heads):
            for way in (RIGHT, LEFT):
                hop(way, step - 1, h).wait_recv()
                hop(way, step, h).start()
            attend(h, [whole_block(way, step, h, hots[way]) for way in (RIGHT, LEFT)])
        return carry

    lax.fori_loop(1, whole, body, 0)

    across = lax.broadcasted_iota(jnp.int32, (LANES, LANES), 1)
    down = lax.broadcasted_iota(jnp.int32, (LANES, LANES), 0)
    same = shift(across, jnp.int32(3)) == shift(down, jnp.int32(3))
    before_it = jnp.where(same & (down < across), 1.0, 0.0).astype(jnp.bfloat16)
    rank_row = jnp.dot(marks[0].astype(jnp.bfloat16), before_it, preferred_element_type=jnp.float32)
    mark_row = marks[0]
    weight = jnp.where(same & (across < down), 1.0, jnp.where(across == down, float(PICKED), 0.0))
    ones = jnp.ones((LANES, LANES), jnp.bfloat16)
    for n in (2, 3):
        mark_hop(n).wait_recv()
    for n in range(1 + len(NEAR)):
        for h in range(heads):
            tables[n, h] = jnp.dot((weight * marks[n, h:h + 1, :]).astype(jnp.bfloat16), ones,
                                   preferred_element_type=jnp.float32)

    hots = [one_hot(source(way, whole)) for way in (RIGHT, LEFT)]
    for h in range(heads):
        for way in (RIGHT, LEFT):
            hop(way, whole - 1, h).wait_recv()
            for part in (K, V):
                def on_whole(way=way, part=part, h=h):
                    whole_part(way, part, h).start()

                def as_packs(way=way, part=part, h=h):
                    make_packs(way, part, SHORT, h, whole)
                    pair_hop(way, part, SHORT, h).start()

                either(goes_far(way, part, h, source(way, whole)), on_whole, as_packs)
        attend(h, [whole_block(way, whole, h, hots[way]) for way in (RIGHT, LEFT)])

    for h in range(heads):
        for way in (RIGHT, LEFT):
            for part in (K, V):
                def from_whole(way=way, part=part, h=h):
                    whole_part(way, part, h).wait_recv()
                    make_packs(way, part, LONG, h, whole + 1)
                    pair_hop(way, part, LONG, h).start()
                    mine[way, part] = pick(0, h, source(way, whole + 1), ring[way, whole + 1, h, part])

                def from_pair(way=way, part=part, h=h):
                    pair_hop(way, part, SHORT, h).wait_recv()
                    single_hop(way, part, SHORT, h).start()
                    mine[way, part] = pairs[way, part, SHORT, h, 0]

                either(goes_far(way, part, h, source(way, whole + 1)), from_whole, from_pair)
        attend_packs(h, source(RIGHT, whole + 1), source(LEFT, whole + 1))

    for h in range(heads):
        for way in (RIGHT, LEFT):
            for part in (K, V):
                def from_pair(way=way, part=part, h=h):
                    pair_hop(way, part, LONG, h).wait_recv()
                    single_hop(way, part, LONG, h).start()
                    mine[way, part] = pairs[way, part, LONG, h, 0]

                def from_single(way=way, part=part, h=h):
                    single_hop(way, part, SHORT, h).wait_recv()
                    mine[way, part] = single[way, part, SHORT, h]

                either(goes_far(way, part, h, source(way, whole + 2)), from_pair, from_single)
        attend_packs(h, source(RIGHT, whole + 2), source(LEFT, whole + 2))

    for n in range(len(NEAR)):
        mark_hop(n).wait_send()
    for h in range(heads):
        for way in (RIGHT, LEFT):
            hop(way, 0, h).wait_send()
            for part in (K, V):
                either(goes_far(way, part, h, source(way, whole)),
                       whole_part(way, part, h).wait_send, pair_hop(way, part, SHORT, h).wait_send)
                either(goes_far(way, part, h, source(way, whole + 1)),
                       pair_hop(way, part, LONG, h).wait_send, single_hop(way, part, SHORT, h).wait_send)

    def drain(step, carry):
        for way in (RIGHT, LEFT):
            for h in range(heads):
                hop(way, step, h).wait_send()
        return carry

    lax.fori_loop(1, whole, drain, 0)

    empty = jnp.zeros((CUBE_TOK, depth), jnp.bfloat16)
    opposite = away(half)
    for h in range(heads):
        hot = jnp.concatenate([pack_hot(h, opposite), jnp.ones((CUBE_TOK, LANES), jnp.bfloat16)], axis=0)
        for part in (K, V):
            def from_left_side(part=part, h=h):
                single_hop(RIGHT, part, LONG, h).wait_recv()
                mine[RIGHT, part] = single[RIGHT, part, LONG, h]

            def from_right_side(part=part, h=h):
                single_hop(LEFT, part, LONG, h).wait_recv()
                mine[RIGHT, part] = single[LEFT, part, LONG, h]

            either(goes_far(RIGHT, part, h, opposite), from_left_side, from_right_side)
        keys = jnp.concatenate([mine[RIGHT, K], empty], axis=0)
        values = jnp.concatenate([mine[RIGHT, V], empty], axis=0)
        attend(h, [(jnp.concatenate([keys, hot], axis=1), values)])
        total = jnp.sum(tot[h], axis=1, keepdims=True)
        out_ref[:, h * depth:(h + 1) * depth] = (acc[h] / total).astype(out_ref.dtype)

    for h in range(heads):
        for way in (RIGHT, LEFT):
            for part in (K, V):
                pl.when(goes_far(way, part, h, source(way, whole + 2)))(single_hop(way, part, LONG, h).wait_send)


def body(ring_size, queries, keys, values, indices):
    heads, cubes, picks = indices.shape
    rows, width = queries.shape
    depth = width // heads
    half = ring_size // 2
    pack = KEEP * CUBE_TOK
    hbm = pl.BlockSpec(memory_space=pl.ANY)
    return pl.pallas_call(
        functools.partial(kernel, ring_size),
        out_shape=jax.ShapeDtypeStruct((rows, width), queries.dtype),
        in_specs=[hbm] * 4,
        out_specs=pl.BlockSpec(memory_space=pltpu.VMEM),
        scratch_shapes=[
            pltpu.VMEM((heads, rows, depth + LANES), jnp.bfloat16),
            pltpu.VMEM((2, half - 1, heads, 2, rows, depth), jnp.bfloat16),
            pltpu.VMEM((2, 2, 2, heads, 2, pack, depth), jnp.bfloat16),
            pltpu.VMEM((2, 2, 2, heads, 2, pack, depth), jnp.bfloat16),
            pltpu.VMEM((2, 2, 2, heads, pack, depth), jnp.bfloat16),
            pltpu.VMEM((2, 2, pack, depth), jnp.bfloat16),
            pltpu.VMEM((1 + len(NEAR), 8, LANES), jnp.float32),
            pltpu.VMEM((1 + len(NEAR), heads, LANES, LANES), jnp.float32),
            pltpu.VMEM((heads, cubes, picks), jnp.int32),
            pltpu.VMEM((heads, rows, depth), jnp.float32),
            pltpu.VMEM((heads, rows, LANES), jnp.float32),
            pltpu.VMEM((heads, rows, LANES), jnp.float32),
            pltpu.SemaphoreType.DMA((heads,)),
            pltpu.SemaphoreType.DMA((heads, 2)),
            pltpu.SemaphoreType.DMA,
            pltpu.SemaphoreType.DMA((len(NEAR),)),
            pltpu.SemaphoreType.DMA((len(NEAR),)),
            pltpu.SemaphoreType.DMA((2, half - 3, heads)),
            pltpu.SemaphoreType.DMA((2, half - 3, heads)),
            pltpu.SemaphoreType.DMA((2, 2, heads, 5)),
            pltpu.SemaphoreType.DMA((2, 2, heads, 5)),
        ],
        compiler_params=pltpu.CompilerParams(
            collective_id=0, has_side_effects=True, vmem_limit_bytes=LIMIT),
        cost_estimate=pl.CostEstimate(
            flops=4 * rows * rows * ring_size * width,
            bytes_accessed=8 * rows * width,
            transcendentals=rows * rows * ring_size * heads),
        name="ring_attention",
    )(queries, keys, values, indices)


def solution(mesh):
    placed = (
        P(("dp", "seq"), "head"),
        P(("dp", "seq"), "head"),
        P(("dp", "seq"), "head"),
        P("head", ("dp", "seq"), None),
    )
    return jax.shard_map(
        functools.partial(body, mesh.shape["seq"]), mesh=mesh, in_specs=placed,
        out_specs=P(("dp", "seq"), "head"), check_vma=False,
    )
```

```python
import functools
import math

import jax
import jax.numpy as jnp
from jax import lax
from jax.experimental import pallas as pl
from jax.experimental.pallas import tpu as pltpu
from jax.sharding import PartitionSpec as P

CUBE_TOK = 64
LIMIT = 56 * 2 ** 20
LANES = 128
MASKED = -1e30
KEEP = 3
PICKED = 16
NEAR = (1, -1, 2, -2)
RIGHT, LEFT = 0, 1
K, V = 0, 1
SHORT, LONG = 0, 1
LEFT_FIRST = 5
FAR_RIGHT = ((0x1856, 0xDFFC, 0xD95C), (0xE062, 0x8463, 0x9222))


def kernel(ring_size, q_hbm, k_hbm, v_hbm, idx_hbm, out_ref,
           q_aug, ring, stage, pairs, single, mine, marks, tables, idx_ref, acc, top, tot,
           q_sem, kv_sem, idx_sem, mark_send, mark_recv, full_send, full_recv, pack_send, pack_recv):
    heads, cubes, picks = idx_ref.shape
    rows = q_hbm.shape[0]
    depth = q_hbm.shape[1] // heads
    half = ring_size // 2
    whole = half - 3
    factor = math.log2(math.e) / math.sqrt(depth)
    me = lax.axis_index("seq")
    early = jnp.where(me < LEFT_FIRST, LEFT, RIGHT)
    ways = (early, 1 - early)

    def away(distance):
        return lax.rem(me + distance + ring_size, ring_size)

    def source(way, distance):
        return away(distance * (2 * way - 1))

    def target(way):
        return {"seq": away(1 - 2 * way)}

    barrier = pltpu.get_barrier_semaphore()
    for distance in (1, -1):
        pl.semaphore_signal(barrier, inc=1, device_id={"seq": away(distance)},
                            device_id_type=pl.DeviceIdType.MESH)

    idx_load = pltpu.make_async_copy(idx_hbm, idx_ref, idx_sem)
    idx_load.start()
    loads = []
    for h in range(heads):
        columns = pl.ds(h * depth, depth)
        for part, ref in ((0, k_hbm), (1, v_hbm)):
            loads.append(pltpu.make_async_copy(
                ref.at[:, columns], ring.at[RIGHT, 0, h, part], kv_sem.at[h, part]))
            loads[-1].start()
    q_loads = []
    for h in range(heads):
        q_loads.append(pltpu.make_async_copy(
            q_hbm.at[:, pl.ds(h * depth, depth)], q_aug.at[h, :, pl.ds(0, depth)], q_sem.at[h]))
        q_loads[-1].start()

    def remote(src, dst, sends, recvs, device):
        return pltpu.make_async_remote_copy(
            src_ref=src, dst_ref=dst, send_sem=sends, recv_sem=recvs,
            device_id=device, device_id_type=pl.DeviceIdType.MESH)

    def hop(way, step, h):
        first = isinstance(step, int) and step == 0
        return remote(ring.at[RIGHT if first else way, step, h], ring.at[way, step + 1, h],
                      full_send.at[way, step, h], full_recv.at[way, step, h], target(way))

    def goes_far(way, part, h, owner):
        bit = lax.rem(lax.shift_right_logical(jnp.int32(FAR_RIGHT[part][h]), owner), 2)
        return bit == 1 - way

    def whole_part(way, part, h):
        return remote(ring.at[way, whole, h, part], ring.at[way, whole + 1, h, part],
                      pack_send.at[way, part, h, 2], pack_recv.at[way, part, h, 2], target(way))

    def pair_hop(way, part, kind, h):
        return remote(stage.at[way, part, kind, h], pairs.at[way, part, kind, h],
                      pack_send.at[way, part, h, kind], pack_recv.at[way, part, h, kind], target(way))

    def single_hop(way, part, kind, h):
        return remote(pairs.at[way, part, kind, h, 1], single.at[way, part, kind, h],
                      pack_send.at[way, part, h, 3 + kind], pack_recv.at[way, part, h, 3 + kind], target(way))

    def mark_hop(n):
        return remote(marks.at[0 if n < 2 else 1 + ((n - 2) ^ 1)], marks.at[1 + (n ^ 1)],
                      mark_send.at[n], mark_recv.at[n], {"seq": away(NEAR[n % 2])})

    pl.semaphore_wait(barrier, 2)
    for h in range(heads):
        loads[2 * h].wait()
        loads[2 * h + 1].wait()
        hop(RIGHT, 0, h).start()
        hop(LEFT, 0, h).start()

    lanes = lax.broadcasted_iota(jnp.int32, (cubes, LANES), 1)
    idx_load.wait()
    marks[0] = jnp.zeros(marks.shape[1:], jnp.float32)
    for h in range(heads):
        chosen = idx_ref[h]
        hit = jnp.zeros((cubes, LANES), jnp.float32)
        for j in range(picks):
            hit = jnp.where(chosen[:, j:j + 1] == lanes, 1.0, hit)
        marks[0, h:h + 1, :] = jnp.max(hit, axis=0, keepdims=True)
        bias = jnp.where(hit > 0.5, 0.0, MASKED)
        for c in range(cubes):
            q_aug[h, c * CUBE_TOK:(c + 1) * CUBE_TOK, depth:] = jnp.broadcast_to(
                bias[c:c + 1, :], (CUBE_TOK, LANES)).astype(q_aug.dtype)
    for n in (0, 1):
        mark_hop(n).start()
    top[...] = jnp.full(top.shape, MASKED, jnp.float32)
    tot[...] = jnp.zeros(tot.shape, jnp.float32)
    acc[...] = jnp.zeros(acc.shape, jnp.float32)

    shift = lax.shift_right_logical
    key_cube = shift(lax.broadcasted_iota(jnp.int32, (rows, LANES), 0), jnp.int32(6))
    key_lane = lax.broadcasted_iota(jnp.int32, (rows, LANES), 1)

    def one_hot(owner):
        return jnp.where(key_lane == key_cube + owner * cubes, 1.0, 0.0).astype(jnp.bfloat16)

    tile = min(rows, 256)

    def attend(h, blocks):
        for r in range(0, rows, tile):
            part = pl.ds(r, tile)
            scores = [
                lax.dot_general(q_aug[h, part, :], key, (((1,), (1,)), ((), ())),
                                preferred_element_type=jnp.float32)
                for key, _ in blocks
            ]
            peak = functools.reduce(
                jnp.maximum, [jnp.max(s, axis=1, keepdims=True) for s in scores])
            before = top[h, part, :]
            after = jnp.maximum(before, peak)
            scale = jnp.exp2((before - after) * factor)
            total = tot[h, part, :] * scale
            mixed = acc[h, part, :] * scale
            for s, (_, value) in zip(scores, blocks):
                pieces = []
                for c in range(0, s.shape[1], LANES):
                    w = jnp.exp2((s[:, c:c + LANES] - after) * factor)
                    total = total + w
                    pieces.append(w.astype(jnp.bfloat16))
                mixed = mixed + jnp.dot(jnp.concatenate(pieces, axis=1), value,
                                        preferred_element_type=jnp.float32)
            top[h, part, :] = after
            tot[h, part, :] = total
            acc[h, part, :] = mixed

    def whole_block(way, step, h, hot):
        return (jnp.concatenate([ring[way, step, h, 0], hot], axis=1), ring[way, step, h, 1])

    for h in range(heads):
        q_loads[h].wait()
    hot_own = one_hot(me)
    for h in range(heads):
        attend(h, [whole_block(RIGHT, 0, h, hot_own)])

    def pick(n, h, owner, block):
        table = tables[n, h, pl.ds(pl.multiple_of(owner * cubes, cubes), cubes), :]
        out = [jnp.zeros((CUBE_TOK, depth), jnp.float32) for _ in range(KEEP)]
        for c in range(cubes):
            cube = block[c * CUBE_TOK:(c + 1) * CUBE_TOK, :].astype(jnp.float32)
            for r in range(KEEP):
                out[r] = jnp.where(table[c:c + 1, :] == float(PICKED + r), cube, out[r])
        return jnp.concatenate(out, axis=0).astype(jnp.bfloat16)

    lane = lax.broadcasted_iota(jnp.int32, (1, LANES), 1)

    def pack_hot(h, owner):
        inside = (shift(lane, jnp.int32(3)) == owner) & (mark_row[h:h + 1, :] > 0.5)
        out = []
        for r in range(KEEP):
            hot = jnp.where(inside & (rank_row[h:h + 1, :] == float(r)), 1.0, 0.0)
            found = jnp.max(hot, axis=1, keepdims=True)
            out.append(jnp.broadcast_to(jnp.where(found > 0.5, hot, 1.0), (CUBE_TOK, LANES)))
        return jnp.concatenate(out, axis=0).astype(jnp.bfloat16)

    def make_packs(way, part, kind, h, distance):
        owner = source(way, distance)
        block = ring[way, distance, h, part]
        first = 1 + way
        stage[way, part, kind, h, 0] = pick(first, h, owner, block)
        stage[way, part, kind, h, 1] = pick(first + 2, h, owner, block)

    def either(condition, first, second):
        pl.when(condition)(first)
        pl.when(jnp.logical_not(condition))(second)

    def attend_packs(h, near, far):
        keys = jnp.concatenate([mine[RIGHT, K], mine[LEFT, K]], axis=0)
        values = jnp.concatenate([mine[RIGHT, V], mine[LEFT, V]], axis=0)
        hot = jnp.concatenate([pack_hot(h, near), pack_hot(h, far)], axis=0)
        attend(h, [(jnp.concatenate([keys, hot], axis=1), values)])

    def body(step, carry):
        @pl.when(step == 2)
        def _():
            for n in (0, 1):
                mark_hop(n).wait_recv()
            for n in (2, 3):
                mark_hop(n).start()

        hots = [one_hot(source(way, step)) for way in (RIGHT, LEFT)]
        for h in range(heads):
            for way in ways:
                hop(way, step - 1, h).wait_recv()
                hop(way, step, h).start()
            attend(h, [whole_block(way, step, h, hots[way]) for way in (RIGHT, LEFT)])
        return carry

    lax.fori_loop(1, whole, body, 0)

    across = lax.broadcasted_iota(jnp.int32, (LANES, LANES), 1)
    down = lax.broadcasted_iota(jnp.int32, (LANES, LANES), 0)
    same = shift(across, jnp.int32(3)) == shift(down, jnp.int32(3))
    before_it = jnp.where(same & (down < across), 1.0, 0.0).astype(jnp.bfloat16)
    rank_row = jnp.dot(marks[0].astype(jnp.bfloat16), before_it, preferred_element_type=jnp.float32)
    mark_row = marks[0]
    weight = jnp.where(same & (across < down), 1.0, jnp.where(across == down, float(PICKED), 0.0))
    ones = jnp.ones((LANES, LANES), jnp.bfloat16)
    for n in (2, 3):
        mark_hop(n).wait_recv()
    for n in range(1 + len(NEAR)):
        for h in range(heads):
            tables[n, h] = jnp.dot((weight * marks[n, h:h + 1, :]).astype(jnp.bfloat16), ones,
                                   preferred_element_type=jnp.float32)

    hots = [one_hot(source(way, whole)) for way in (RIGHT, LEFT)]
    for h in range(heads):
        for way in ways:
            hop(way, whole - 1, h).wait_recv()
            for part in (K, V):
                def on_whole(way=way, part=part, h=h):
                    whole_part(way, part, h).start()

                def as_packs(way=way, part=part, h=h):
                    make_packs(way, part, SHORT, h, whole)
                    pair_hop(way, part, SHORT, h).start()

                either(goes_far(way, part, h, source(way, whole)), on_whole, as_packs)
        attend(h, [whole_block(way, whole, h, hots[way]) for way in (RIGHT, LEFT)])

    for h in range(heads):
        for way in ways:
            for part in (K, V):
                def from_whole(way=way, part=part, h=h):
                    whole_part(way, part, h).wait_recv()
                    make_packs(way, part, LONG, h, whole + 1)
                    pair_hop(way, part, LONG, h).start()
                    mine[way, part] = pick(0, h, source(way, whole + 1), ring[way, whole + 1, h, part])

                def from_pair(way=way, part=part, h=h):
                    pair_hop(way, part, SHORT, h).wait_recv()
                    single_hop(way, part, SHORT, h).start()
                    mine[way, part] = pairs[way, part, SHORT, h, 0]

                either(goes_far(way, part, h, source(way, whole + 1)), from_whole, from_pair)
        attend_packs(h, source(RIGHT, whole + 1), source(LEFT, whole + 1))

    for h in range(heads):
        for way in ways:
            for part in (K, V):
                def from_pair(way=way, part=part, h=h):
                    pair_hop(way, part, LONG, h).wait_recv()
                    single_hop(way, part, LONG, h).start()
                    mine[way, part] = pairs[way, part, LONG, h, 0]

                def from_single(way=way, part=part, h=h):
                    single_hop(way, part, SHORT, h).wait_recv()
                    mine[way, part] = single[way, part, SHORT, h]

                either(goes_far(way, part, h, source(way, whole + 2)), from_pair, from_single)
        attend_packs(h, source(RIGHT, whole + 2), source(LEFT, whole + 2))

    for n in range(len(NEAR)):
        mark_hop(n).wait_send()
    for h in range(heads):
        for way in (RIGHT, LEFT):
            hop(way, 0, h).wait_send()
            for part in (K, V):
                either(goes_far(way, part, h, source(way, whole)),
                       whole_part(way, part, h).wait_send, pair_hop(way, part, SHORT, h).wait_send)
                either(goes_far(way, part, h, source(way, whole + 1)),
                       pair_hop(way, part, LONG, h).wait_send, single_hop(way, part, SHORT, h).wait_send)

    def drain(step, carry):
        for way in (RIGHT, LEFT):
            for h in range(heads):
                hop(way, step, h).wait_send()
        return carry

    lax.fori_loop(1, whole, drain, 0)

    empty = jnp.zeros((CUBE_TOK, depth), jnp.bfloat16)
    opposite = away(half)
    for h in range(heads):
        hot = jnp.concatenate([pack_hot(h, opposite), jnp.ones((CUBE_TOK, LANES), jnp.bfloat16)], axis=0)
        for part in (K, V):
            def from_left_side(part=part, h=h):
                single_hop(RIGHT, part, LONG, h).wait_recv()
                mine[RIGHT, part] = single[RIGHT, part, LONG, h]

            def from_right_side(part=part, h=h):
                single_hop(LEFT, part, LONG, h).wait_recv()
                mine[RIGHT, part] = single[LEFT, part, LONG, h]

            either(goes_far(RIGHT, part, h, opposite), from_left_side, from_right_side)
        keys = jnp.concatenate([mine[RIGHT, K], empty], axis=0)
        values = jnp.concatenate([mine[RIGHT, V], empty], axis=0)
        attend(h, [(jnp.concatenate([keys, hot], axis=1), values)])
        total = jnp.sum(tot[h], axis=1, keepdims=True)
        out_ref[:, h * depth:(h + 1) * depth] = (acc[h] / total).astype(out_ref.dtype)

    for h in range(heads):
        for way in (RIGHT, LEFT):
            for part in (K, V):
                pl.when(goes_far(way, part, h, source(way, whole + 2)))(single_hop(way, part, LONG, h).wait_send)


def body(ring_size, queries, keys, values, indices):
    heads, cubes, picks = indices.shape
    rows, width = queries.shape
    depth = width // heads
    half = ring_size // 2
    pack = KEEP * CUBE_TOK
    hbm = pl.BlockSpec(memory_space=pl.ANY)
    return pl.pallas_call(
        functools.partial(kernel, ring_size),
        out_shape=pltpu.VMEM((rows, width), queries.dtype),
        in_specs=[hbm] * 4,
        out_specs=pl.BlockSpec(memory_space=pltpu.VMEM),
        scratch_shapes=[
            pltpu.VMEM((heads, rows, depth + LANES), jnp.bfloat16),
            pltpu.VMEM((2, half - 1, heads, 2, rows, depth), jnp.bfloat16),
            pltpu.VMEM((2, 2, 2, heads, 2, pack, depth), jnp.bfloat16),
            pltpu.VMEM((2, 2, 2, heads, 2, pack, depth), jnp.bfloat16),
            pltpu.VMEM((2, 2, 2, heads, pack, depth), jnp.bfloat16),
            pltpu.VMEM((2, 2, pack, depth), jnp.bfloat16),
            pltpu.VMEM((1 + len(NEAR), 8, LANES), jnp.float32),
            pltpu.VMEM((1 + len(NEAR), heads, LANES, LANES), jnp.float32),
            pltpu.VMEM((heads, cubes, picks), jnp.int32),
            pltpu.VMEM((heads, rows, depth), jnp.float32),
            pltpu.VMEM((heads, rows, LANES), jnp.float32),
            pltpu.VMEM((heads, rows, LANES), jnp.float32),
            pltpu.SemaphoreType.DMA((heads,)),
            pltpu.SemaphoreType.DMA((heads, 2)),
            pltpu.SemaphoreType.DMA,
            pltpu.SemaphoreType.DMA((len(NEAR),)),
            pltpu.SemaphoreType.DMA((len(NEAR),)),
            pltpu.SemaphoreType.DMA((2, half - 3, heads)),
            pltpu.SemaphoreType.DMA((2, half - 3, heads)),
            pltpu.SemaphoreType.DMA((2, 2, heads, 5)),
            pltpu.SemaphoreType.DMA((2, 2, heads, 5)),
        ],
        compiler_params=pltpu.CompilerParams(
            collective_id=0, has_side_effects=True, vmem_limit_bytes=LIMIT),
        cost_estimate=pl.CostEstimate(
            flops=4 * rows * rows * ring_size * width,
            bytes_accessed=8 * rows * width,
            transcendentals=rows * rows * ring_size * heads),
        name="ring_attention",
    )(queries, keys, values, indices)


def solution(mesh):
    placed = (
        P(("dp", "seq"), "head"),
        P(("dp", "seq"), "head"),
        P(("dp", "seq"), "head"),
        P("head", ("dp", "seq"), None),
    )
    return jax.shard_map(
        functools.partial(body, mesh.shape["seq"]), mesh=mesh, in_specs=placed,
        out_specs=P(("dp", "seq"), "head"), check_vma=False,
    )
```

```python
import functools
import math

import jax
import jax.numpy as jnp
from jax import lax
from jax.experimental import pallas as pl
from jax.experimental.pallas import tpu as pltpu
from jax.sharding import PartitionSpec as P

CUBE_TOK = 64
LIMIT = 56 * 2 ** 20
LANES = 128
MASKED = -1e30
KEEP = 3
PICKED = 16
NEAR = (1, -1, 2, -2)
RIGHT, LEFT = 0, 1
K, V = 0, 1
SHORT, LONG = 0, 1
LEFT_FIRST = 5
FAR_RIGHT = ((0x6073, 0xE973, 0x4123), (0x5CCC, 0x9CCC, 0xBC88))


def kernel(ring_size, q_hbm, k_hbm, v_hbm, idx_hbm, out_ref,
           q_aug, ring, stage, pairs, single, mine, marks, tables, idx_ref, acc, top, tot,
           q_sem, kv_sem, idx_sem, mark_send, mark_recv, full_send, full_recv, pack_send, pack_recv,
           answer_right, answer_left):
    heads, cubes, picks = idx_ref.shape
    rows = q_hbm.shape[0]
    depth = q_hbm.shape[1] // heads
    half = ring_size // 2
    whole = half - 3
    factor = math.log2(math.e) / math.sqrt(depth)
    me = lax.axis_index("seq")
    early = jnp.where(me < LEFT_FIRST, LEFT, RIGHT)
    ways = (early, 1 - early)

    def away(distance):
        return lax.rem(me + distance + ring_size, ring_size)

    def source(way, distance):
        return away(distance * (2 * way - 1))

    def target(way):
        return {"seq": away(1 - 2 * way)}

    first_one, last_one, late = me == 0, me == ring_size - 1, me >= half

    def tell(semaphore, distance):
        pl.semaphore_signal(semaphore, inc=1, device_id={"seq": away(distance)},
                            device_id_type=pl.DeviceIdType.MESH)

    barrier = pltpu.get_barrier_semaphore()

    @pl.when(jnp.logical_not(last_one))
    def _():
        tell(barrier, 1)

    @pl.when(first_one | (me > half))
    def _():
        tell(barrier, -1)

    idx_load = pltpu.make_async_copy(idx_hbm, idx_ref, idx_sem)
    idx_load.start()
    loads = []
    for h in range(heads):
        columns = pl.ds(h * depth, depth)
        for part, ref in ((0, k_hbm), (1, v_hbm)):
            loads.append(pltpu.make_async_copy(
                ref.at[:, columns], ring.at[RIGHT, 0, h, part], kv_sem.at[h, part]))
            loads[-1].start()
    q_loads = []
    for h in range(heads):
        q_loads.append(pltpu.make_async_copy(
            q_hbm.at[:, pl.ds(h * depth, depth)], q_aug.at[h, :, pl.ds(0, depth)], q_sem.at[h]))
        q_loads[-1].start()

    def remote(src, dst, sends, recvs, device):
        return pltpu.make_async_remote_copy(
            src_ref=src, dst_ref=dst, send_sem=sends, recv_sem=recvs,
            device_id=device, device_id_type=pl.DeviceIdType.MESH)

    def hop(way, step, h):
        first = isinstance(step, int) and step == 0
        return remote(ring.at[RIGHT if first else way, step, h], ring.at[way, step + 1, h],
                      full_send.at[way, step, h], full_recv.at[way, step, h], target(way))

    def goes_far(way, part, h, owner):
        bit = lax.rem(lax.shift_right_logical(jnp.int32(FAR_RIGHT[part][h]), owner), 2)
        return bit == 1 - way

    def whole_part(way, part, h):
        return remote(ring.at[way, whole, h, part], ring.at[way, whole + 1, h, part],
                      pack_send.at[way, part, h, 2], pack_recv.at[way, part, h, 2], target(way))

    def pair_hop(way, part, kind, h):
        return remote(stage.at[way, part, kind, h], pairs.at[way, part, kind, h],
                      pack_send.at[way, part, h, kind], pack_recv.at[way, part, h, kind], target(way))

    def single_hop(way, part, kind, h):
        return remote(pairs.at[way, part, kind, h, 1], single.at[way, part, kind, h],
                      pack_send.at[way, part, h, 3 + kind], pack_recv.at[way, part, h, 3 + kind], target(way))

    def mark_hop(n):
        return remote(marks.at[0 if n < 2 else 1 + ((n - 2) ^ 1)], marks.at[1 + (n ^ 1)],
                      mark_send.at[n], mark_recv.at[n], {"seq": away(NEAR[n % 2])})

    @pl.when(jnp.logical_not(first_one))
    def _():
        pl.semaphore_wait(barrier, jnp.where(late, 2, 1))

    @pl.when(jnp.logical_not(first_one) & (me <= half))
    def _():
        tell(answer_right, -1)

    @pl.when(last_one)
    def _():
        tell(answer_left, 1)

    for load in loads:
        load.wait()

    @pl.when(late)
    def _():
        for h in range(heads):
            hop(RIGHT, 0, h).start()
            hop(LEFT, 0, h).start()

    @pl.when(jnp.logical_not(late))
    def _():
        @pl.when(jnp.logical_not(first_one))
        def _():
            for h in range(heads):
                hop(LEFT, 0, h).start()

        pl.semaphore_wait(answer_right, 1)
        for h in range(heads):
            hop(RIGHT, 0, h).start()

    lanes = lax.broadcasted_iota(jnp.int32, (cubes, LANES), 1)
    idx_load.wait()
    marks[0] = jnp.zeros(marks.shape[1:], jnp.float32)
    for h in range(heads):
        chosen = idx_ref[h]
        hit = jnp.zeros((cubes, LANES), jnp.float32)
        for j in range(picks):
            hit = jnp.where(chosen[:, j:j + 1] == lanes, 1.0, hit)
        marks[0, h:h + 1, :] = jnp.max(hit, axis=0, keepdims=True)
        bias = jnp.where(hit > 0.5, 0.0, MASKED)
        for c in range(cubes):
            q_aug[h, c * CUBE_TOK:(c + 1) * CUBE_TOK, depth:] = jnp.broadcast_to(
                bias[c:c + 1, :], (CUBE_TOK, LANES)).astype(q_aug.dtype)
    top[...] = jnp.full(top.shape, MASKED, jnp.float32)
    tot[...] = jnp.zeros(tot.shape, jnp.float32)
    acc[...] = jnp.zeros(acc.shape, jnp.float32)

    shift = lax.shift_right_logical
    key_cube = shift(lax.broadcasted_iota(jnp.int32, (rows, LANES), 0), jnp.int32(6))
    key_lane = lax.broadcasted_iota(jnp.int32, (rows, LANES), 1)

    def one_hot(owner):
        return jnp.where(key_lane == key_cube + owner * cubes, 1.0, 0.0).astype(jnp.bfloat16)

    tile = min(rows, 256)

    def attend(h, blocks):
        for r in range(0, rows, tile):
            part = pl.ds(r, tile)
            scores = [
                lax.dot_general(q_aug[h, part, :], key, (((1,), (1,)), ((), ())),
                                preferred_element_type=jnp.float32)
                for key, _ in blocks
            ]
            peak = functools.reduce(
                jnp.maximum, [jnp.max(s, axis=1, keepdims=True) for s in scores])
            before = top[h, part, :]
            after = jnp.maximum(before, peak)
            scale = jnp.exp2((before - after) * factor)
            total = tot[h, part, :] * scale
            mixed = acc[h, part, :] * scale
            for s, (_, value) in zip(scores, blocks):
                pieces = []
                for c in range(0, s.shape[1], LANES):
                    w = jnp.exp2((s[:, c:c + LANES] - after) * factor)
                    total = total + w
                    pieces.append(w.astype(jnp.bfloat16))
                mixed = mixed + jnp.dot(jnp.concatenate(pieces, axis=1), value,
                                        preferred_element_type=jnp.float32)
            top[h, part, :] = after
            tot[h, part, :] = total
            acc[h, part, :] = mixed

    def whole_block(way, step, h, hot):
        return (jnp.concatenate([ring[way, step, h, 0], hot], axis=1), ring[way, step, h, 1])

    for h in range(heads):
        q_loads[h].wait()
    hot_own = one_hot(me)
    for h in range(heads):
        attend(h, [whole_block(RIGHT, 0, h, hot_own)])

    def pick(n, h, owner, block):
        table = tables[n, h, pl.ds(pl.multiple_of(owner * cubes, cubes), cubes), :]
        out = [jnp.zeros((CUBE_TOK, depth), jnp.float32) for _ in range(KEEP)]
        for c in range(cubes):
            cube = block[c * CUBE_TOK:(c + 1) * CUBE_TOK, :].astype(jnp.float32)
            for r in range(KEEP):
                out[r] = jnp.where(table[c:c + 1, :] == float(PICKED + r), cube, out[r])
        return jnp.concatenate(out, axis=0).astype(jnp.bfloat16)

    lane = lax.broadcasted_iota(jnp.int32, (1, LANES), 1)

    def pack_hot(h, owner):
        inside = (shift(lane, jnp.int32(3)) == owner) & (mark_row[h:h + 1, :] > 0.5)
        out = []
        for r in range(KEEP):
            hot = jnp.where(inside & (rank_row[h:h + 1, :] == float(r)), 1.0, 0.0)
            found = jnp.max(hot, axis=1, keepdims=True)
            out.append(jnp.broadcast_to(jnp.where(found > 0.5, hot, 1.0), (CUBE_TOK, LANES)))
        return jnp.concatenate(out, axis=0).astype(jnp.bfloat16)

    def make_packs(way, part, kind, h, distance):
        owner = source(way, distance)
        block = ring[way, distance, h, part]
        first = 1 + way
        stage[way, part, kind, h, 0] = pick(first, h, owner, block)
        stage[way, part, kind, h, 1] = pick(first + 2, h, owner, block)

    def either(condition, first, second):
        pl.when(condition)(first)
        pl.when(jnp.logical_not(condition))(second)

    def attend_packs(h, near, far):
        keys = jnp.concatenate([mine[RIGHT, K], mine[LEFT, K]], axis=0)
        values = jnp.concatenate([mine[RIGHT, V], mine[LEFT, V]], axis=0)
        hot = jnp.concatenate([pack_hot(h, near), pack_hot(h, far)], axis=0)
        attend(h, [(jnp.concatenate([keys, hot], axis=1), values)])

    @pl.when(first_one)
    def _():
        pl.semaphore_wait(answer_left, 1)
        for h in range(heads):
            hop(LEFT, 0, h).start()

    for n in (0, 1):
        mark_hop(n).start()

    def body(step, carry):
        @pl.when(step == 2)
        def _():
            for n in (0, 1):
                mark_hop(n).wait_recv()
            for n in (2, 3):
                mark_hop(n).start()

        hots = [one_hot(source(way, step)) for way in (RIGHT, LEFT)]
        for h in range(heads):
            for way in ways:
                hop(way, step - 1, h).wait_recv()
                hop(way, step, h).start()
            attend(h, [whole_block(way, step, h, hots[way]) for way in (RIGHT, LEFT)])
        return carry

    lax.fori_loop(1, whole, body, 0)

    across = lax.broadcasted_iota(jnp.int32, (LANES, LANES), 1)
    down = lax.broadcasted_iota(jnp.int32, (LANES, LANES), 0)
    same = shift(across, jnp.int32(3)) == shift(down, jnp.int32(3))
    before_it = jnp.where(same & (down < across), 1.0, 0.0).astype(jnp.bfloat16)
    rank_row = jnp.dot(marks[0].astype(jnp.bfloat16), before_it, preferred_element_type=jnp.float32)
    mark_row = marks[0]
    weight = jnp.where(same & (across < down), 1.0, jnp.where(across == down, float(PICKED), 0.0))
    ones = jnp.ones((LANES, LANES), jnp.bfloat16)
    for n in (2, 3):
        mark_hop(n).wait_recv()
    for n in range(1 + len(NEAR)):
        for h in range(heads):
            tables[n, h] = jnp.dot((weight * marks[n, h:h + 1, :]).astype(jnp.bfloat16), ones,
                                   preferred_element_type=jnp.float32)

    hots = [one_hot(source(way, whole)) for way in (RIGHT, LEFT)]
    for h in range(heads):
        for way in ways:
            hop(way, whole - 1, h).wait_recv()
            for part in (K, V):
                def on_whole(way=way, part=part, h=h):
                    whole_part(way, part, h).start()

                def as_packs(way=way, part=part, h=h):
                    make_packs(way, part, SHORT, h, whole)
                    pair_hop(way, part, SHORT, h).start()

                either(goes_far(way, part, h, source(way, whole)), on_whole, as_packs)
        attend(h, [whole_block(way, whole, h, hots[way]) for way in (RIGHT, LEFT)])

    for h in range(heads):
        for way in ways:
            for part in (K, V):
                def from_whole(way=way, part=part, h=h):
                    whole_part(way, part, h).wait_recv()
                    make_packs(way, part, LONG, h, whole + 1)
                    pair_hop(way, part, LONG, h).start()
                    mine[way, part] = pick(0, h, source(way, whole + 1), ring[way, whole + 1, h, part])

                def from_pair(way=way, part=part, h=h):
                    pair_hop(way, part, SHORT, h).wait_recv()
                    single_hop(way, part, SHORT, h).start()
                    mine[way, part] = pairs[way, part, SHORT, h, 0]

                either(goes_far(way, part, h, source(way, whole + 1)), from_whole, from_pair)
        attend_packs(h, source(RIGHT, whole + 1), source(LEFT, whole + 1))

    for h in range(heads):
        for way in ways:
            for part in (K, V):
                def from_pair(way=way, part=part, h=h):
                    pair_hop(way, part, LONG, h).wait_recv()
                    single_hop(way, part, LONG, h).start()
                    mine[way, part] = pairs[way, part, LONG, h, 0]

                def from_single(way=way, part=part, h=h):
                    single_hop(way, part, SHORT, h).wait_recv()
                    mine[way, part] = single[way, part, SHORT, h]

                either(goes_far(way, part, h, source(way, whole + 2)), from_pair, from_single)
        attend_packs(h, source(RIGHT, whole + 2), source(LEFT, whole + 2))

    for n in range(len(NEAR)):
        mark_hop(n).wait_send()
    for h in range(heads):
        for way in (RIGHT, LEFT):
            hop(way, 0, h).wait_send()
            for part in (K, V):
                either(goes_far(way, part, h, source(way, whole)),
                       whole_part(way, part, h).wait_send, pair_hop(way, part, SHORT, h).wait_send)
                either(goes_far(way, part, h, source(way, whole + 1)),
                       pair_hop(way, part, LONG, h).wait_send, single_hop(way, part, SHORT, h).wait_send)

    def drain(step, carry):
        for way in (RIGHT, LEFT):
            for h in range(heads):
                hop(way, step, h).wait_send()
        return carry

    lax.fori_loop(1, whole, drain, 0)

    empty = jnp.zeros((CUBE_TOK, depth), jnp.bfloat16)
    opposite = away(half)
    for h in range(heads):
        hot = jnp.concatenate([pack_hot(h, opposite), jnp.ones((CUBE_TOK, LANES), jnp.bfloat16)], axis=0)
        for part in (K, V):
            def from_left_side(part=part, h=h):
                single_hop(RIGHT, part, LONG, h).wait_recv()
                mine[RIGHT, part] = single[RIGHT, part, LONG, h]

            def from_right_side(part=part, h=h):
                single_hop(LEFT, part, LONG, h).wait_recv()
                mine[RIGHT, part] = single[LEFT, part, LONG, h]

            either(goes_far(RIGHT, part, h, opposite), from_left_side, from_right_side)
        keys = jnp.concatenate([mine[RIGHT, K], empty], axis=0)
        values = jnp.concatenate([mine[RIGHT, V], empty], axis=0)
        attend(h, [(jnp.concatenate([keys, hot], axis=1), values)])
        total = jnp.sum(tot[h], axis=1, keepdims=True)
        out_ref[:, h * depth:(h + 1) * depth] = (acc[h] / total).astype(out_ref.dtype)

    for h in range(heads):
        for way in (RIGHT, LEFT):
            for part in (K, V):
                pl.when(goes_far(way, part, h, source(way, whole + 2)))(single_hop(way, part, LONG, h).wait_send)


def body(ring_size, queries, keys, values, indices):
    heads, cubes, picks = indices.shape
    rows, width = queries.shape
    depth = width // heads
    half = ring_size // 2
    pack = KEEP * CUBE_TOK
    hbm = pl.BlockSpec(memory_space=pl.ANY)
    return pl.pallas_call(
        functools.partial(kernel, ring_size),
        out_shape=pltpu.VMEM((rows, width), queries.dtype),
        in_specs=[hbm] * 4,
        out_specs=pl.BlockSpec(memory_space=pltpu.VMEM),
        scratch_shapes=[
            pltpu.VMEM((heads, rows, depth + LANES), jnp.bfloat16),
            pltpu.VMEM((2, half - 1, heads, 2, rows, depth), jnp.bfloat16),
            pltpu.VMEM((2, 2, 2, heads, 2, pack, depth), jnp.bfloat16),
            pltpu.VMEM((2, 2, 2, heads, 2, pack, depth), jnp.bfloat16),
            pltpu.VMEM((2, 2, 2, heads, pack, depth), jnp.bfloat16),
            pltpu.VMEM((2, 2, pack, depth), jnp.bfloat16),
            pltpu.VMEM((1 + len(NEAR), 8, LANES), jnp.float32),
            pltpu.VMEM((1 + len(NEAR), heads, LANES, LANES), jnp.float32),
            pltpu.VMEM((heads, cubes, picks), jnp.int32),
            pltpu.VMEM((heads, rows, depth), jnp.float32),
            pltpu.VMEM((heads, rows, LANES), jnp.float32),
            pltpu.VMEM((heads, rows, LANES), jnp.float32),
            pltpu.SemaphoreType.DMA((heads,)),
            pltpu.SemaphoreType.DMA((heads, 2)),
            pltpu.SemaphoreType.DMA,
            pltpu.SemaphoreType.DMA((len(NEAR),)),
            pltpu.SemaphoreType.DMA((len(NEAR),)),
            pltpu.SemaphoreType.DMA((2, half - 3, heads)),
            pltpu.SemaphoreType.DMA((2, half - 3, heads)),
            pltpu.SemaphoreType.DMA((2, 2, heads, 5)),
            pltpu.SemaphoreType.DMA((2, 2, heads, 5)),
            pltpu.SemaphoreType.REGULAR,
            pltpu.SemaphoreType.REGULAR,
        ],
        compiler_params=pltpu.CompilerParams(
            collective_id=0, has_side_effects=True, vmem_limit_bytes=LIMIT),
        cost_estimate=pl.CostEstimate(
            flops=4 * rows * rows * ring_size * width,
            bytes_accessed=8 * rows * width,
            transcendentals=rows * rows * ring_size * heads),
        name="ring_attention",
    )(queries, keys, values, indices)


def solution(mesh):
    placed = (
        P(("dp", "seq"), "head"),
        P(("dp", "seq"), "head"),
        P(("dp", "seq"), "head"),
        P("head", ("dp", "seq"), None),
    )
    return jax.shard_map(
        functools.partial(body, mesh.shape["seq"]), mesh=mesh, in_specs=placed,
        out_specs=P(("dp", "seq"), "head"), check_vma=False,
    )
```

```python
import functools
import math

import jax
import jax.numpy as jnp
from jax import lax
from jax.experimental import pallas as pl
from jax.experimental.pallas import tpu as pltpu
from jax.sharding import PartitionSpec as P

CUBE_TOK = 64
LIMIT = 56 * 2 ** 20
LANES = 128
MASKED = -1e30
KEEP = 3
PICKED = 16
NEAR = (1, -1, 2, -2)
RIGHT, LEFT = 0, 1
K, V = 0, 1
SHORT, LONG = 0, 1
LEFT_FIRST = 5
FAR_RIGHT = ((0x1856, 0xDFFC, 0xD95C), (0xE062, 0x8463, 0x9222))


def kernel(ring_size, q_hbm, k_hbm, v_hbm, idx_hbm, out_ref,
           q_aug, ring, stage, pairs, single, mine, marks, tables, idx_ref, acc, top, tot,
           q_sem, kv_sem, idx_sem, mark_send, mark_recv, full_send, full_recv, pack_send, pack_recv):
    heads, cubes, picks = idx_ref.shape
    rows = q_hbm.shape[0]
    depth = q_hbm.shape[1] // heads
    half = ring_size // 2
    whole = half - 3
    factor = math.log2(math.e) / math.sqrt(depth)
    me = lax.axis_index("seq")
    early = jnp.where(me < LEFT_FIRST, LEFT, RIGHT)
    ways = (early, 1 - early)

    def away(distance):
        return lax.rem(me + distance + ring_size, ring_size)

    def source(way, distance):
        return away(distance * (2 * way - 1))

    def target(way):
        return {"seq": away(1 - 2 * way)}

    barrier = pltpu.get_barrier_semaphore()
    for distance in (1, -1):
        pl.semaphore_signal(barrier, inc=1, device_id={"seq": away(distance)},
                            device_id_type=pl.DeviceIdType.MESH)

    idx_load = pltpu.make_async_copy(idx_hbm, idx_ref, idx_sem)
    idx_load.start()
    loads = []
    for h in range(heads):
        columns = pl.ds(h * depth, depth)
        for part, ref in ((0, k_hbm), (1, v_hbm)):
            loads.append(pltpu.make_async_copy(
                ref.at[:, columns], ring.at[RIGHT, 0, h, part], kv_sem.at[h, part]))
            loads[-1].start()
    q_loads = []
    for h in range(heads):
        q_loads.append(pltpu.make_async_copy(
            q_hbm.at[:, pl.ds(h * depth, depth)], q_aug.at[h, :, pl.ds(0, depth)], q_sem.at[h]))
        q_loads[-1].start()

    def remote(src, dst, sends, recvs, device):
        return pltpu.make_async_remote_copy(
            src_ref=src, dst_ref=dst, send_sem=sends, recv_sem=recvs,
            device_id=device, device_id_type=pl.DeviceIdType.MESH)

    def hop(way, step, h):
        first = isinstance(step, int) and step == 0
        return remote(ring.at[RIGHT if first else way, step, h], ring.at[way, step + 1, h],
                      full_send.at[way, step, h], full_recv.at[way, step, h], target(way))

    def goes_far(way, part, h, owner):
        bit = lax.rem(lax.shift_right_logical(jnp.int32(FAR_RIGHT[part][h]), owner), 2)
        return bit == 1 - way

    def whole_part(way, part, h):
        return remote(ring.at[way, whole, h, part], ring.at[way, whole + 1, h, part],
                      pack_send.at[way, part, h, 2], pack_recv.at[way, part, h, 2], target(way))

    def pair_hop(way, part, kind, h):
        return remote(stage.at[way, part, kind, h], pairs.at[way, part, kind, h],
                      pack_send.at[way, part, h, kind], pack_recv.at[way, part, h, kind], target(way))

    def single_hop(way, part, kind, h):
        return remote(pairs.at[way, part, kind, h, 1], single.at[way, part, kind, h],
                      pack_send.at[way, part, h, 3 + kind], pack_recv.at[way, part, h, 3 + kind], target(way))

    def mark_hop(n):
        return remote(marks.at[0 if n < 2 else 1 + ((n - 2) ^ 1)], marks.at[1 + (n ^ 1)],
                      mark_send.at[n], mark_recv.at[n], {"seq": away(NEAR[n % 2])})

    pl.semaphore_wait(barrier, 2)
    for h in range(heads):
        loads[2 * h].wait()
        loads[2 * h + 1].wait()
        hop(RIGHT, 0, h).start()
        hop(LEFT, 0, h).start()

    lanes = lax.broadcasted_iota(jnp.int32, (cubes, LANES), 1)
    idx_load.wait()
    marks[0] = jnp.zeros(marks.shape[1:], jnp.float32)
    for h in range(heads):
        chosen = idx_ref[h]
        hit = jnp.zeros((cubes, LANES), jnp.float32)
        for j in range(picks):
            hit = jnp.where(chosen[:, j:j + 1] == lanes, 1.0, hit)
        marks[0, h:h + 1, :] = jnp.max(hit, axis=0, keepdims=True)
        bias = jnp.where(hit > 0.5, 0.0, MASKED)
        for c in range(cubes):
            q_aug[h, c * CUBE_TOK:(c + 1) * CUBE_TOK, depth:] = jnp.broadcast_to(
                bias[c:c + 1, :], (CUBE_TOK, LANES)).astype(q_aug.dtype)
    for n in (0, 1):
        mark_hop(n).start()
    top[...] = jnp.full(top.shape, MASKED, jnp.float32)
    tot[...] = jnp.zeros(tot.shape, jnp.float32)
    acc[...] = jnp.zeros(acc.shape, jnp.float32)

    shift = lax.shift_right_logical
    key_cube = shift(lax.broadcasted_iota(jnp.int32, (rows, LANES), 0), jnp.int32(6))
    key_lane = lax.broadcasted_iota(jnp.int32, (rows, LANES), 1)

    def one_hot(owner):
        return jnp.where(key_lane == key_cube + owner * cubes, 1.0, 0.0).astype(jnp.bfloat16)

    tile = min(rows, 256)

    def attend(h, blocks):
        for r in range(0, rows, tile):
            part = pl.ds(r, tile)
            scores = [
                lax.dot_general(q_aug[h, part, :], key, (((1,), (1,)), ((), ())),
                                preferred_element_type=jnp.float32)
                for key, _ in blocks
            ]
            peak = functools.reduce(
                jnp.maximum, [jnp.max(s, axis=1, keepdims=True) for s in scores])
            before = top[h, part, :]
            after = jnp.maximum(before, peak)
            scale = jnp.exp2((before - after) * factor)
            total = tot[h, part, :] * scale
            mixed = acc[h, part, :] * scale
            for s, (_, value) in zip(scores, blocks):
                pieces = []
                for c in range(0, s.shape[1], LANES):
                    w = jnp.exp2((s[:, c:c + LANES] - after) * factor)
                    total = total + w
                    pieces.append(w.astype(jnp.bfloat16))
                mixed = mixed + jnp.dot(jnp.concatenate(pieces, axis=1), value,
                                        preferred_element_type=jnp.float32)
            top[h, part, :] = after
            tot[h, part, :] = total
            acc[h, part, :] = mixed

    def whole_block(way, step, h, hot):
        return (jnp.concatenate([ring[way, step, h, 0], hot], axis=1), ring[way, step, h, 1])

    for h in range(heads):
        q_loads[h].wait()
    hot_own = one_hot(me)
    for h in range(heads):
        attend(h, [whole_block(RIGHT, 0, h, hot_own)])

    def pick(n, h, owner, block):
        table = tables[n, h, pl.ds(pl.multiple_of(owner * cubes, cubes), cubes), :]
        out = [jnp.zeros((CUBE_TOK, depth), jnp.float32) for _ in range(KEEP)]
        for c in range(cubes):
            cube = block[c * CUBE_TOK:(c + 1) * CUBE_TOK, :].astype(jnp.float32)
            for r in range(KEEP):
                out[r] = jnp.where(table[c:c + 1, :] == float(PICKED + r), cube, out[r])
        return jnp.concatenate(out, axis=0).astype(jnp.bfloat16)

    lane = lax.broadcasted_iota(jnp.int32, (1, LANES), 1)

    def pack_hot(h, owner):
        inside = (shift(lane, jnp.int32(3)) == owner) & (mark_row[h:h + 1, :] > 0.5)
        out = []
        for r in range(KEEP):
            hot = jnp.where(inside & (rank_row[h:h + 1, :] == float(r)), 1.0, 0.0)
            found = jnp.max(hot, axis=1, keepdims=True)
            out.append(jnp.broadcast_to(jnp.where(found > 0.5, hot, 1.0), (CUBE_TOK, LANES)))
        return jnp.concatenate(out, axis=0).astype(jnp.bfloat16)

    def make_packs(way, part, kind, h, distance):
        owner = source(way, distance)
        block = ring[way, distance, h, part]
        first = 1 + way
        stage[way, part, kind, h, 0] = pick(first, h, owner, block)
        stage[way, part, kind, h, 1] = pick(first + 2, h, owner, block)

    def either(condition, first, second):
        pl.when(condition)(first)
        pl.when(jnp.logical_not(condition))(second)

    def attend_packs(h, near, far):
        keys = jnp.concatenate([mine[RIGHT, K], mine[LEFT, K]], axis=0)
        values = jnp.concatenate([mine[RIGHT, V], mine[LEFT, V]], axis=0)
        hot = jnp.concatenate([pack_hot(h, near), pack_hot(h, far)], axis=0)
        attend(h, [(jnp.concatenate([keys, hot], axis=1), values)])

    def body(step, carry):
        @pl.when(step == 2)
        def _():
            for n in (0, 1):
                mark_hop(n).wait_recv()
            for n in (2, 3):
                mark_hop(n).start()

        hots = [one_hot(source(way, step)) for way in (RIGHT, LEFT)]
        for h in range(heads):
            for way in ways:
                hop(way, step - 1, h).wait_recv()
                hop(way, step, h).start()
            attend(h, [whole_block(way, step, h, hots[way]) for way in (RIGHT, LEFT)])
        return carry

    lax.fori_loop(1, whole, body, 0)

    across = lax.broadcasted_iota(jnp.int32, (LANES, LANES), 1)
    down = lax.broadcasted_iota(jnp.int32, (LANES, LANES), 0)
    same = shift(across, jnp.int32(3)) == shift(down, jnp.int32(3))
    before_it = jnp.where(same & (down < across), 1.0, 0.0).astype(jnp.bfloat16)
    rank_row = jnp.dot(marks[0].astype(jnp.bfloat16), before_it, preferred_element_type=jnp.float32)
    mark_row = marks[0]
    weight = jnp.where(same & (across < down), 1.0, jnp.where(across == down, float(PICKED), 0.0))
    ones = jnp.ones((LANES, LANES), jnp.bfloat16)
    for n in (2, 3):
        mark_hop(n).wait_recv()
    for n in range(1 + len(NEAR)):
        for h in range(heads):
            tables[n, h] = jnp.dot((weight * marks[n, h:h + 1, :]).astype(jnp.bfloat16), ones,
                                   preferred_element_type=jnp.float32)

    hots = [one_hot(source(way, whole)) for way in (RIGHT, LEFT)]
    for h in range(heads):
        for way in ways:
            hop(way, whole - 1, h).wait_recv()
            for part in (K, V):
                def on_whole(way=way, part=part, h=h):
                    whole_part(way, part, h).start()

                def as_packs(way=way, part=part, h=h):
                    make_packs(way, part, SHORT, h, whole)
                    pair_hop(way, part, SHORT, h).start()

                either(goes_far(way, part, h, source(way, whole)), on_whole, as_packs)
        attend(h, [whole_block(way, whole, h, hots[way]) for way in (RIGHT, LEFT)])

    for h in range(heads):
        for way in ways:
            for part in (K, V):
                def from_whole(way=way, part=part, h=h):
                    whole_part(way, part, h).wait_recv()
                    make_packs(way, part, LONG, h, whole + 1)
                    pair_hop(way, part, LONG, h).start()
                    mine[way, part] = pick(0, h, source(way, whole + 1), ring[way, whole + 1, h, part])

                def from_pair(way=way, part=part, h=h):
                    pair_hop(way, part, SHORT, h).wait_recv()
                    single_hop(way, part, SHORT, h).start()
                    mine[way, part] = pairs[way, part, SHORT, h, 0]

                either(goes_far(way, part, h, source(way, whole + 1)), from_whole, from_pair)
        attend_packs(h, source(RIGHT, whole + 1), source(LEFT, whole + 1))

    for h in range(heads):
        for way in ways:
            for part in (K, V):
                def from_pair(way=way, part=part, h=h):
                    pair_hop(way, part, LONG, h).wait_recv()
                    single_hop(way, part, LONG, h).start()
                    mine[way, part] = pairs[way, part, LONG, h, 0]

                def from_single(way=way, part=part, h=h):
                    single_hop(way, part, SHORT, h).wait_recv()
                    mine[way, part] = single[way, part, SHORT, h]

                either(goes_far(way, part, h, source(way, whole + 2)), from_pair, from_single)
        attend_packs(h, source(RIGHT, whole + 2), source(LEFT, whole + 2))

    for n in range(len(NEAR)):
        mark_hop(n).wait_send()
    for h in range(heads):
        for way in (RIGHT, LEFT):
            hop(way, 0, h).wait_send()
            for part in (K, V):
                either(goes_far(way, part, h, source(way, whole)),
                       whole_part(way, part, h).wait_send, pair_hop(way, part, SHORT, h).wait_send)
                either(goes_far(way, part, h, source(way, whole + 1)),
                       pair_hop(way, part, LONG, h).wait_send, single_hop(way, part, SHORT, h).wait_send)

    def drain(step, carry):
        for way in (RIGHT, LEFT):
            for h in range(heads):
                hop(way, step, h).wait_send()
        return carry

    lax.fori_loop(1, whole, drain, 0)

    empty = jnp.zeros((CUBE_TOK, depth), jnp.bfloat16)
    opposite = away(half)
    for h in range(heads):
        hot = jnp.concatenate([pack_hot(h, opposite), jnp.ones((CUBE_TOK, LANES), jnp.bfloat16)], axis=0)
        for part in (K, V):
            def from_left_side(part=part, h=h):
                single_hop(RIGHT, part, LONG, h).wait_recv()
                mine[RIGHT, part] = single[RIGHT, part, LONG, h]

            def from_right_side(part=part, h=h):
                single_hop(LEFT, part, LONG, h).wait_recv()
                mine[RIGHT, part] = single[LEFT, part, LONG, h]

            either(goes_far(RIGHT, part, h, opposite), from_left_side, from_right_side)
        keys = jnp.concatenate([mine[RIGHT, K], empty], axis=0)
        values = jnp.concatenate([mine[RIGHT, V], empty], axis=0)
        attend(h, [(jnp.concatenate([keys, hot], axis=1), values)])
        total = jnp.sum(tot[h], axis=1, keepdims=True)
        out_ref[:, h * depth:(h + 1) * depth] = (acc[h] / total).astype(out_ref.dtype)

    for h in range(heads):
        for way in (RIGHT, LEFT):
            for part in (K, V):
                pl.when(goes_far(way, part, h, source(way, whole + 2)))(single_hop(way, part, LONG, h).wait_send)


def hand_out(result, out, sem):
    copy = pltpu.make_async_copy(result, out, sem)
    copy.start()
    copy.wait()


def body(ring_size, queries, keys, values, indices):
    heads, cubes, picks = indices.shape
    rows, width = queries.shape
    depth = width // heads
    half = ring_size // 2
    pack = KEEP * CUBE_TOK
    hbm = pl.BlockSpec(memory_space=pl.ANY)
    attended = pl.pallas_call(
        functools.partial(kernel, ring_size),
        out_shape=pltpu.VMEM((rows, width), queries.dtype),
        in_specs=[hbm] * 4,
        out_specs=pl.BlockSpec(memory_space=pltpu.VMEM),
        scratch_shapes=[
            pltpu.VMEM((heads, rows, depth + LANES), jnp.bfloat16),
            pltpu.VMEM((2, half - 1, heads, 2, rows, depth), jnp.bfloat16),
            pltpu.VMEM((2, 2, 2, heads, 2, pack, depth), jnp.bfloat16),
            pltpu.VMEM((2, 2, 2, heads, 2, pack, depth), jnp.bfloat16),
            pltpu.VMEM((2, 2, 2, heads, pack, depth), jnp.bfloat16),
            pltpu.VMEM((2, 2, pack, depth), jnp.bfloat16),
            pltpu.VMEM((1 + len(NEAR), 8, LANES), jnp.float32),
            pltpu.VMEM((1 + len(NEAR), heads, LANES, LANES), jnp.float32),
            pltpu.VMEM((heads, cubes, picks), jnp.int32),
            pltpu.VMEM((heads, rows, depth), jnp.float32),
            pltpu.VMEM((heads, rows, LANES), jnp.float32),
            pltpu.VMEM((heads, rows, LANES), jnp.float32),
            pltpu.SemaphoreType.DMA((heads,)),
            pltpu.SemaphoreType.DMA((heads, 2)),
            pltpu.SemaphoreType.DMA,
            pltpu.SemaphoreType.DMA((len(NEAR),)),
            pltpu.SemaphoreType.DMA((len(NEAR),)),
            pltpu.SemaphoreType.DMA((2, half - 3, heads)),
            pltpu.SemaphoreType.DMA((2, half - 3, heads)),
            pltpu.SemaphoreType.DMA((2, 2, heads, 5)),
            pltpu.SemaphoreType.DMA((2, 2, heads, 5)),
        ],
        compiler_params=pltpu.CompilerParams(
            collective_id=0, has_side_effects=True, vmem_limit_bytes=LIMIT),
        cost_estimate=pl.CostEstimate(
            flops=4 * rows * rows * ring_size * width,
            bytes_accessed=8 * rows * width,
            transcendentals=rows * rows * ring_size * heads),
        name="ring_attention",
    )(queries, keys, values, indices)
    return pl.pallas_call(
        hand_out,
        out_shape=jax.ShapeDtypeStruct((rows, width), queries.dtype),
        in_specs=[pl.BlockSpec(memory_space=pltpu.VMEM)],
        out_specs=hbm,
        scratch_shapes=[pltpu.SemaphoreType.DMA],
        cost_estimate=pl.CostEstimate(flops=0, bytes_accessed=2 * rows * width, transcendentals=0),
        name="hand_out",
    )(attended)


def solution(mesh):
    placed = (
        P(("dp", "seq"), "head"),
        P(("dp", "seq"), "head"),
        P(("dp", "seq"), "head"),
        P("head", ("dp", "seq"), None),
    )
    return jax.shard_map(
        functools.partial(body, mesh.shape["seq"]), mesh=mesh, in_specs=placed,
        out_specs=P(("dp", "seq"), "head"), check_vma=False,
    )
```
